256 devices in a mesh: expert: 32 (over y_hi, z, core), dp: 8 (over x, y_lo).
Axes of the slice: x: 4, y: 4 (y_hi: 2, y_lo: 2; y = y_hi * 2 + y_lo), z: 8, core: 2. Of those that a mesh axis runs over, the one named last changes fastest.
Arguments:
- tokens: bfloat16 [32768, 2048], P(('expert', 'dp')), may hold values from -6 to 6
- out_grad: bfloat16 [32768, 2048], P(('expert', 'dp')), may hold values from -0.0059814453 to 0.0059814453
- saved_pre: bfloat16 [32768, 8, 1024], P(('expert', 'dp')), may hold values from -6 to 6
- router_weight: float32 [2048, 64], replicated, may hold values from -0.125 to 0.125
- slot_expert: int32 [256], replicated, may hold values from 0 to 63, as said below
- slot_of: int32 [32768, 8], P(('expert', 'dp')), may hold values from 0 to 255, as said below
- slot_weight: bfloat16 [256, 2048, 1536], P(('expert', 'dp')), as said below
Outputs:
- token_grad: bfloat16 [32768, 2048], P(('expert', 'dp'))
- expert_grads: bfloat16 [2048, 64, 1536], P('dp', 'expert')
- router_grad: float32 [2048, 64], replicated
The draws below stay inside these ranges and needn't reach their ends.
Inputs may be any that keep to these rules, and one draw needn't show every extreme that they name: `slot_expert`: slots 8 * c to 8 * c + 7 hold experts 2 c and 2 c + 1, each on at least one slot; one of the two holds the lower slots of the group, the other the higher ones. `slot_of`: the 8 slots of a token lie in distinct groups of 8 slots. The 128 tokens of one device name each group exactly 32 times and no slot more than 5 times; in every group one slot is named exactly 5 times by every device's tokens. `slot_weight`: slots that hold the same expert hold the same weights.
All inputs are finite; a program needn't handle non-finite values.
Results may differ from the reference program's by a relative error of at most 0.01.
Values may be sent and summed in bfloat16 or wider, within the bound.
A program may use at most 128 MiB of HBM per device.

```python
import jax
import jax.numpy as jnp
from jax import lax

D = 2048
FFW = 512
TOP = 8
TOK_DEV = 128
EXPERTS = 64
SLOTS = 256
TOKENS = 32768
CAP = 5
N_EXPERT = 32
N_DP = 8
DEVICES = 256


def slot_table(key):
    replicas = jax.random.randint(jax.random.fold_in(key, 901), (N_EXPERT,), 1, N_DP, dtype=jnp.int32)
    flips = jax.random.randint(jax.random.fold_in(key, 902), (N_EXPERT,), 0, 2, dtype=jnp.int32)
    slot_ids = jnp.arange(SLOTS, dtype=jnp.int32)
    column = slot_ids // N_DP
    upper = (slot_ids % N_DP >= replicas[column]).astype(jnp.int32)
    return (2 * column + (upper + flips[column]) % 2).astype(jnp.int32)


def draw_slot_expert(key, part):
    placed = slot_table(key)
    return placed


def draw_slot_of(key, part):
    key = jax.random.fold_in(key, 5)
    hottest = jax.random.randint(jax.random.fold_in(key, 1), (N_EXPERT,), 0, N_DP, dtype=jnp.int32)
    block_keys = jax.random.split(jax.random.fold_in(key, 2), DEVICES)

    def one_block(block_key):
        first_key, second_key = jax.random.split(block_key)
        column_perm = jax.random.permutation(first_key, N_EXPERT).astype(jnp.int32)
        token_perm = jax.random.permutation(second_key, TOK_DEV).astype(jnp.int32)
        flat = jnp.arange(TOK_DEV * TOP, dtype=jnp.int32)
        column = column_perm[flat % N_EXPERT]
        arrival = flat // N_EXPERT
        spill = (hottest[column] + 1 + (arrival - CAP) % (N_DP - 1)) % N_DP
        data_slot = jnp.where(arrival < CAP, hottest[column], spill)
        chosen = (column * N_DP + data_slot).reshape(TOK_DEV, TOP)
        return chosen[token_perm]
    return jax.vmap(one_block)(block_keys).reshape(TOKENS, TOP).astype(jnp.int32)


def draw_slot_weight(key, part):
    placed = slot_table(key)
    key = jax.random.fold_in(key, 7)
    column_scale = jnp.where(jnp.arange(3 * FFW) < 2 * FFW, D ** (-0.5), FFW ** (-0.5)).astype(jnp.float32)

    def one_slot(expert):
        expert_key = jax.random.fold_in(key, expert)
        values = jax.random.normal(expert_key, (D, 3 * FFW), jnp.float32)
        return (values * column_scale[None, :]).astype(jnp.bfloat16)
    return jax.lax.map(one_slot, placed)


def block_scale(key, extent, shards, smallest, high):
    def one(axis_at, parts):
        heights = jax.random.uniform(jax.random.fold_in(jax.random.fold_in(key, 6), axis_at), (parts,), jnp.float32, smallest / len(shards), high / len(shards))
        return jnp.repeat(jnp.exp(heights), extent[axis_at] // parts).reshape((-1,) + (1,) * (len(extent) - axis_at - 1))

    factor_of = one(*shards[0])
    for cut in shards[1:]:
        factor_of = factor_of * one(*cut)
    return factor_of


def scatter_about(key, extent, scale, most, shards=(), kind=jnp.bfloat16):
    level = block_scale(key, extent, shards, -0.22, 0.18) if shards else 1.0
    array = jax.random.normal(key, extent, jnp.float32) * scale * level
    return jnp.minimum(jnp.maximum(array, -most), most).astype(kind)


def setup_inputs(seed: int = 0) -> dict:
    keys = jax.random.split(jax.random.key(seed), 8)
    tokens = scatter_about(keys[0], (TOKENS, D), 1.0, 6.0, ((0, 256),))
    out_grad = scatter_about(keys[1], (TOKENS, D), 0.001, 0.0059814453, ((0, 256),))
    saved_pre = scatter_about(keys[2], (TOKENS, TOP, 2 * FFW), 1.0, 6.0, ((0, 256),))
    router_weight = scatter_about(keys[3], (D, EXPERTS), D ** -0.5, 0.125, (), jnp.float32)
    slot_expert = draw_slot_expert(jax.random.fold_in(keys[7], 71), 0)
    slot_of = draw_slot_of(jax.random.fold_in(keys[7], 71), 0)
    slot_weight = draw_slot_weight(jax.random.fold_in(keys[7], 71), 0)
    return dict(tokens=tokens, out_grad=out_grad, saved_pre=saved_pre, router_weight=router_weight, slot_expert=slot_expert, slot_of=slot_of, slot_weight=slot_weight)


zloss_coef = 0.001
balance_coef = 0.01


def expert_rows(inputs, upstream, saved_rows, route_weight, matrix):
    hidden_width = saved_rows.shape[1] // 2
    gate_pre = saved_rows[:, :hidden_width].astype(jnp.float32)
    upward = saved_rows[:, hidden_width:].astype(jnp.float32)
    sigmoid_gate = jax.nn.sigmoid(gate_pre)
    active = gate_pre * sigmoid_gate
    hidden = active * upward
    weight_col = route_weight.astype(jnp.float32)[:, None]
    back_grad = jnp.dot(upstream, matrix[:, 2 * hidden_width:], preferred_element_type=jnp.float32)
    prob_grad = jnp.sum(back_grad * hidden, axis=1).astype(jnp.bfloat16)
    scaled = (weight_col * hidden).astype(jnp.bfloat16)
    hidden_grad = weight_col * back_grad
    gate_grad = hidden_grad * upward * sigmoid_gate * (1.0 + gate_pre * (1.0 - sigmoid_gate))
    pre_grad = jnp.concatenate([gate_grad, hidden_grad * active], axis=1).astype(jnp.bfloat16)
    part_grad = lax.dot_general(pre_grad, matrix[:, :2 * hidden_width], (((1,), (1,)), ((), ())),
                                preferred_element_type=jnp.float32).astype(jnp.bfloat16)
    return part_grad, prob_grad, pre_grad, scaled


def slot_gradient(inputs, upstream, pre_grad, scaled):
    first = lax.dot_general(inputs, pre_grad, (((0,), (0,)), ((), ())), preferred_element_type=jnp.float32)
    second = lax.dot_general(upstream, scaled, (((0,), (0,)), ((), ())), preferred_element_type=jnp.float32)
    return jnp.concatenate([first, second], axis=1).astype(jnp.bfloat16)


def reference(tokens, out_grad, saved_pre, router_weight, slot_expert, slot_of, slot_weight):
    slot_flat = slot_of.reshape(-1).astype(jnp.int32)
    expert_ids = jnp.take(slot_expert, slot_of, axis=0).astype(jnp.int32)
    wide_tokens = tokens.astype(jnp.float32)
    logits = jnp.dot(wide_tokens, router_weight, precision=lax.Precision.HIGHEST)
    log_total = jax.nn.logsumexp(logits, axis=1)
    router_probs = jnp.exp(logits - log_total[:, None])
    chosen = expert_ids[:, :, None] == jnp.arange(EXPERTS, dtype=jnp.int32)[None, None, :]
    chosen_prob = jnp.sum(jnp.where(chosen, router_probs[:, None, :], 0.0), axis=2).astype(jnp.bfloat16)
    block_counts = jnp.sum(chosen.astype(jnp.int32).reshape(DEVICES, TOK_DEV, TOP, EXPERTS), axis=(1, 2))
    counts = jnp.repeat(block_counts, TOK_DEV, axis=0)
    saved_flat = saved_pre.reshape(TOKENS * TOP, 2 * FFW)
    prob_flat = chosen_prob.reshape(-1)
    row_limit = DEVICES * CAP
    zero_half = jnp.zeros((), jnp.bfloat16)

    def visit(totals, current):
        token_acc, prob_acc, grad_acc = totals
        slot_index, matrix = current
        matches = slot_flat == slot_index
        places = jnp.nonzero(matches, size=row_limit, fill_value=0)[0].astype(jnp.int32)
        usable = jnp.arange(row_limit, dtype=jnp.int32) < jnp.sum(matches.astype(jnp.int32))
        owners = (places // TOP).astype(jnp.int32)
        inputs = jnp.where(usable[:, None], tokens[owners], zero_half)
        upstream = jnp.where(usable[:, None], out_grad[owners], zero_half)
        saved_rows = jnp.where(usable[:, None], saved_flat[places], zero_half)
        route_weight = jnp.where(usable, prob_flat[places], zero_half)
        part_grad, prob_grad, pre_grad, scaled = expert_rows(inputs, upstream, saved_rows, route_weight, matrix)
        slot_grad = lax.optimization_barrier(slot_gradient(inputs, upstream, pre_grad, scaled)).astype(jnp.float32)
        token_acc = token_acc.at[owners].add(jnp.where(usable[:, None], part_grad.astype(jnp.float32), 0.0))
        prob_acc = prob_acc.at[places].add(jnp.where(usable, prob_grad.astype(jnp.float32), 0.0))
        grad_acc = grad_acc.at[slot_expert[slot_index]].add(slot_grad)
        return (token_acc, prob_acc, grad_acc), None

    start_state = (jnp.zeros((TOKENS, D), jnp.float32), jnp.zeros((TOKENS * TOP,), jnp.float32),
                   jnp.zeros((EXPERTS, D, 3 * FFW), jnp.float32))
    (token_acc, prob_acc, grad_acc), _ = lax.scan(visit, start_state,
                                                  (jnp.arange(SLOTS, dtype=jnp.int32), slot_weight))
    prob_tokens = prob_acc.reshape(TOKENS, TOP)
    probs_grad = jnp.sum(jnp.where(chosen, prob_tokens[:, :, None], 0.0), axis=1)
    probs_grad = probs_grad + balance_coef * EXPERTS * counts.astype(jnp.float32) / (TOK_DEV * TOP)
    inner = jnp.sum(router_probs * probs_grad, axis=1, keepdims=True)
    logits_grad = router_probs * (probs_grad - inner) + 2.0 * zloss_coef * log_total[:, None] * router_probs
    router_grad = jnp.dot(wide_tokens.T, logits_grad, precision=lax.Precision.HIGHEST)
    router_part = jnp.dot(logits_grad, router_weight.T, precision=lax.Precision.HIGHEST)
    token_grad = (token_acc + router_part).astype(jnp.bfloat16)
    expert_grads = jnp.transpose(grad_acc, (1, 0, 2)).astype(jnp.bfloat16)
    return token_grad, expert_grads, router_grad
```

```python
import jax
import jax.numpy as jnp
from jax import lax
from jax.experimental import pallas as pl
from jax.experimental.pallas import tpu as pltpu
from jax.sharding import PartitionSpec as P

zloss_coef = 0.001
balance_coef = 0.01
MESH = pl.DeviceIdType.MESH
ANY = pl.BlockSpec(memory_space=pl.ANY)
BF = jnp.bfloat16
F32 = jnp.float32


def greet(ne, nd, with_expert, with_dp):
    e, d = lax.axis_index("expert"), lax.axis_index("dp")
    barrier = pltpu.get_barrier_semaphore()
    total = 0
    if with_expert:
        def one(i, _):
            pl.semaphore_signal(barrier, inc=1, device_id=(lax.rem(e + i, ne), d), device_id_type=MESH)
            return 0
        lax.fori_loop(1, ne, one, 0)
        total += ne - 1
    if with_dp:
        def two(i, _):
            pl.semaphore_signal(barrier, inc=1, device_id=(e, lax.rem(d + i, nd)), device_id_type=MESH)
            return 0
        lax.fori_loop(1, nd, two, 0)
        total += nd - 1
    pl.semaphore_wait(barrier, total)


def send_all(ne, srcs, dsts, send_sem, recv_sem, local_sem):
    e, d = lax.axis_index("expert"), lax.axis_index("dp")
    for n, (src, dst) in enumerate(zip(srcs, dsts)):
        def one(i, _):
            half = (i + 1) // 2
            odd = lax.rem(i, 2)
            off = odd * half + (1 - odd) * (ne - half)
            peer = lax.rem(e + off, ne)
            pltpu.make_async_remote_copy(
                src_ref=src.at[peer], dst_ref=dst.at[e],
                send_sem=send_sem.at[n], recv_sem=recv_sem.at[n],
                device_id=(peer, d), device_id_type=MESH).start()
            return 0
        lax.fori_loop(1, ne, one, 0)
        pltpu.make_async_copy(src.at[e], dst.at[e], local_sem.at[n]).start()


def wait_all(ne, srcs, dsts, send_sem, recv_sem, local_sem):
    e, d = lax.axis_index("expert"), lax.axis_index("dp")
    for n, (src, dst) in enumerate(zip(srcs, dsts)):
        pltpu.make_async_remote_copy(
            src_ref=src.at[pl.ds(0, ne - 1)], dst_ref=dst.at[pl.ds(0, ne - 1)],
            send_sem=send_sem.at[n], recv_sem=recv_sem.at[n],
            device_id=(lax.rem(e + 1, ne), d), device_id_type=MESH).wait()
        pltpu.make_async_copy(src.at[e], dst.at[e], local_sem.at[n]).wait()


def exchange(arrays, ne, nd, collective_id):
    count = len(arrays)

    def kernel(*refs):
        srcs, dsts = refs[:count], refs[count:2 * count]
        send_sem, recv_sem, local_sem = refs[2 * count:]
        greet(ne, nd, True, False)
        send_all(ne, srcs, dsts, send_sem, recv_sem, local_sem)
        wait_all(ne, srcs, dsts, send_sem, recv_sem, local_sem)

    return pl.pallas_call(
        kernel,
        out_shape=[jax.ShapeDtypeStruct(a.shape, a.dtype) for a in arrays],
        in_specs=[ANY] * count, out_specs=[ANY] * count,
        scratch_shapes=[pltpu.SemaphoreType.DMA((count,))] * 3,
        compiler_params=pltpu.CompilerParams(collective_id=collective_id, has_side_effects=True),
    )(*arrays)


def forward_exchange(arrays, weight, ne, nd, collective_id):
    count = len(arrays)
    width, cols = weight.shape
    rows = width // nd

    def kernel(*refs):
        srcs, w = refs[:count], refs[count]
        dsts, both = refs[count + 1:2 * count + 1], refs[2 * count + 1]
        send_sem, recv_sem, local_sem, root_send, piece_sem, y_sem, x_send, x_recv = refs[2 * count + 2:]
        e, d = lax.axis_index("expert"), lax.axis_index("dp")
        greet(ne, nd, True, True)
        for side, root in ((0, 0), (1, nd - 1)):
            @pl.when(d == root)
            def _():
                pltpu.make_async_copy(
                    w.at[pl.ds(root * rows, rows)], both.at[side, root], piece_sem.at[side]).start()
                for j in [1, 7, 2, 6, 3, 5, 4]:
                    q = (root + j) % nd
                    pltpu.make_async_remote_copy(
                        src_ref=w.at[pl.ds(q * rows, rows)], dst_ref=both.at[side, q],
                        send_sem=root_send.at[side], recv_sem=piece_sem.at[side],
                        device_id=(e, q), device_id_type=MESH).start()
        send_all(ne, srcs[:2], dsts[:2], send_sem, recv_sem, local_sem)
        for side in range(2):
            pltpu.make_async_copy(w.at[pl.ds(0, rows)], both.at[side, d], piece_sem.at[side]).wait()
        pair = d + 1 - 2 * lax.rem(d, 2)
        first = lax.rem(d, 2)
        along_y = pltpu.make_async_remote_copy(
            src_ref=both.at[pl.ds(0, 2), d], dst_ref=both.at[pl.ds(0, 2), d],
            send_sem=y_sem.at[0], recv_sem=y_sem.at[1], device_id=(e, pair), device_id_type=MESH)
        along_y.start()
        send_all_rest = (srcs[2:], dsts[2:], send_sem.at[pl.ds(2, count - 2)], recv_sem.at[pl.ds(2, count - 2)],
                         local_sem.at[pl.ds(2, count - 2)])
        along_y.wait()
        duo = (d // 2) * 2
        copies = []
        for k in (1, 3, 2):
            q = lax.rem(d + 2 * k, nd)
            copies.append(pltpu.make_async_remote_copy(
                src_ref=both.at[pl.ds(0, 2), pl.ds(duo, 2)], dst_ref=both.at[pl.ds(0, 2), pl.ds(duo, 2)],
                send_sem=x_send.at[k - 1], recv_sem=x_recv.at[k - 1], device_id=(e, q), device_id_type=MESH))
        for c in copies:
            c.start()
        send_all(ne, *send_all_rest)
        wait_all(ne, srcs, dsts, send_sem, recv_sem, local_sem)
        for c in copies:
            c.wait()
        for side, root in ((0, 0), (1, nd - 1)):
            @pl.when(d == root)
            def _():
                pltpu.make_async_remote_copy(
                    src_ref=both.at[side, pl.ds(0, nd - 1)], dst_ref=both.at[side, pl.ds(0, nd - 1)],
                    send_sem=root_send.at[side], recv_sem=piece_sem.at[side],
                    device_id=(e, (root + 1) % nd), device_id_type=MESH).wait_send()

    return pl.pallas_call(
        kernel,
        out_shape=[jax.ShapeDtypeStruct(a.shape, a.dtype) for a in arrays]
        + [jax.ShapeDtypeStruct((2, nd, rows, cols), weight.dtype)],
        in_specs=[ANY] * (count + 1), out_specs=[ANY] * (count + 1),
        scratch_shapes=[pltpu.SemaphoreType.DMA((count,))] * 3
        + [pltpu.SemaphoreType.DMA((2,))] * 3 + [pltpu.SemaphoreType.DMA((3,))] * 2,
        compiler_params=pltpu.CompilerParams(collective_id=collective_id, has_side_effects=True),
    )(*arrays, weight)


def backward_exchange(part, grad_up, grad_down, router, ne, nd, collective_id):
    width = grad_up.shape[0]
    two = width // (nd // 2)
    one = width // nd
    cu, cd = grad_up.shape[1], grad_down.shape[1]
    rr, rc = router.shape
    rp = rr // nd
    nchip = ne // 2
    rl = rc // nchip

    def kernel(part, gu, gd, router, back, ou, od, orouter,
               bu, bd, keep_u, keep_d, out_u, out_d, in_u, in_d,
               rbuf, racc, rcore, rmine, rpiece, rfull,
               send_sem, recv_sem, local_sem, a_send, a_recv, own_sem, b_send, b_recv,
               r_send, r_recv, fin_sem):
        e, d = lax.axis_index("expert"), lax.axis_index("dp")
        greet(ne, nd, True, True)

        def rs_dp(i, _):
            q = lax.rem(d + i, nd)
            pltpu.make_async_remote_copy(
                src_ref=router.at[pl.ds(pl.multiple_of(q * rp, rp), rp)], dst_ref=rbuf.at[d],
                send_sem=r_send.at[0], recv_sem=r_recv.at[0], device_id=(e, q), device_id_type=MESH).start()
            return 0
        lax.fori_loop(1, nd, rs_dp, 0)
        own_r = pltpu.make_async_copy(router.at[pl.ds(pl.multiple_of(d * rp, rp), rp)], rbuf.at[d], own_sem.at[2])
        own_r.start()

        x, y = d // 2, lax.rem(d, 2)
        copies = []
        for k in (1, 3, 2):
            xq = lax.rem(x + k, nd // 2)
            src_rows = pl.ds(pl.multiple_of(xq * two, two), two)
            for n, (src, dst) in enumerate(((gu, bu), (gd, bd))):
                copies.append(pltpu.make_async_remote_copy(
                    src_ref=src.at[src_rows], dst_ref=dst.at[k - 1],
                    send_sem=a_send.at[k - 1, n], recv_sem=a_recv.at[k - 1, n],
                    device_id=(e, xq * 2 + y), device_id_type=MESH))
        for c in copies:
            c.start()
        my_rows = pl.ds(pl.multiple_of(x * two, two), two)
        own_u = pltpu.make_async_copy(gu.at[my_rows], bu.at[3], own_sem.at[0])
        own_d = pltpu.make_async_copy(gd.at[my_rows], bd.at[3], own_sem.at[1])
        own_u.start()
        own_d.start()
        send_all(ne, [part], [back], send_sem, recv_sem, local_sem)

        own_r.wait()
        pltpu.make_async_remote_copy(
            src_ref=rbuf.at[pl.ds(0, nd - 1)], dst_ref=rbuf.at[pl.ds(0, nd - 1)],
            send_sem=r_send.at[0], recv_sem=r_recv.at[0], device_id=(e, lax.rem(d + 1, nd)),
            device_id_type=MESH).wait()
        racc[...] = jnp.sum(rbuf[...], axis=0)
        mate = e + 1 - 2 * lax.rem(e, 2)
        core = lax.rem(e, 2)
        chip = e // 2
        cc = pltpu.make_async_remote_copy(
            src_ref=racc, dst_ref=rcore, send_sem=r_send.at[1], recv_sem=r_recv.at[1],
            device_id=(mate, d), device_id_type=MESH)
        cc.start()
        cc.wait()
        for n in range(nchip):
            rmine[n] = racc[:, n * rl:(n + 1) * rl] + rcore[:, n * rl:(n + 1) * rl]

        def rs_chip(i, _):
            q = lax.rem(chip + i, nchip)
            pltpu.make_async_remote_copy(
                src_ref=rmine.at[q], dst_ref=rpiece.at[chip], send_sem=r_send.at[2], recv_sem=r_recv.at[2],
                device_id=(q * 2 + core, d), device_id_type=MESH).start()
            return 0
        lax.fori_loop(1, nchip, rs_chip, 0)
        rpiece[chip] = rmine[chip]
        pltpu.make_async_remote_copy(
            src_ref=rpiece.at[pl.ds(0, nchip - 1)], dst_ref=rpiece.at[pl.ds(0, nchip - 1)],
            send_sem=r_send.at[2], recv_sem=r_recv.at[2], device_id=(mate, d), device_id_type=MESH).wait()
        rfull[chip] = jnp.sum(rpiece[...], axis=0)

        def ag_chip(i, _):
            q = lax.rem(chip + i, nchip)
            pltpu.make_async_remote_copy(
                src_ref=rfull.at[chip], dst_ref=rfull.at[chip], send_sem=r_send.at[3], recv_sem=r_recv.at[3],
                device_id=(q * 2 + core, d), device_id_type=MESH).start()
            return 0
        lax.fori_loop(1, nchip, ag_chip, 0)
        pltpu.make_async_remote_copy(
            src_ref=rfull.at[pl.ds(0, nchip - 1)], dst_ref=rfull.at[pl.ds(0, nchip - 1)],
            send_sem=r_send.at[3], recv_sem=r_recv.at[3], device_id=(mate, d), device_id_type=MESH).wait()

        def ag_dp(i, _):
            q = lax.rem(d + i, nd)
            pltpu.make_async_remote_copy(
                src_ref=rfull, dst_ref=orouter.at[d], send_sem=r_send.at[4], recv_sem=r_recv.at[4],
                device_id=(e, q), device_id_type=MESH).start()
            return 0
        lax.fori_loop(1, nd, ag_dp, 0)
        own_f = pltpu.make_async_copy(rfull, orouter.at[d], own_sem.at[3])
        own_f.start()

        own_u.wait()
        own_d.wait()
        for c in copies:
            c.wait()
        for buf, keep, out in ((bu, keep_u, out_u), (bd, keep_d, out_d)):
            def tile(i, _):
                at = pl.multiple_of(i * 16, 16)
                other = pl.multiple_of((1 - y) * one + i * 16, 16)
                total = buf[0, pl.ds(other, 16), :].astype(F32)
                for n in range(1, 4):
                    total = total + buf[n, pl.ds(other, 16), :].astype(F32)
                out[pl.ds(at, 16), :] = total.astype(BF)
                return 0
            lax.fori_loop(0, one // 16, tile, 0)
        pair = d + 1 - 2 * y
        swaps = []
        for n, (src, dst) in enumerate(((out_u, in_u), (out_d, in_d))):
            c = pltpu.make_async_remote_copy(
                src_ref=src, dst_ref=dst, send_sem=b_send.at[n], recv_sem=b_recv.at[n],
                device_id=(e, pair), device_id_type=MESH)
            c.start()
            swaps.append(c)
        for buf, keep, out in ((bu, keep_u, out_u), (bd, keep_d, out_d)):
            def tile(i, _):
                at = pl.multiple_of(i * 16, 16)
                mine = pl.multiple_of(y * one + i * 16, 16)
                total = buf[0, pl.ds(mine, 16), :].astype(F32)
                for n in range(1, 4):
                    total = total + buf[n, pl.ds(mine, 16), :].astype(F32)
                keep[pl.ds(at, 16), :] = total
                return 0
            lax.fori_loop(0, one // 16, tile, 0)
        for c in swaps:
            c.wait()
        for got, keep, out in ((in_u, keep_u, out_u), (in_d, keep_d, out_d)):
            def tile(i, _):
                at = pl.multiple_of(i * 16, 16)
                out[pl.ds(at, 16), :] = (keep[pl.ds(at, 16), :] + got[pl.ds(at, 16), :].astype(F32)).astype(BF)
                return 0
            lax.fori_loop(0, one // 16, tile, 0)
        f1 = pltpu.make_async_copy(out_u, ou, fin_sem.at[0])
        f2 = pltpu.make_async_copy(out_d, od, fin_sem.at[1])
        f1.start()
        f2.start()
        pltpu.make_async_remote_copy(
            src_ref=orouter.at[pl.ds(0, nd - 1)], dst_ref=orouter.at[pl.ds(0, nd - 1)],
            send_sem=r_send.at[4], recv_sem=r_recv.at[4], device_id=(e, lax.rem(d + 1, nd)),
            device_id_type=MESH).wait()
        own_f.wait()
        wait_all(ne, [part], [back], send_sem, recv_sem, local_sem)
        f1.wait()
        f2.wait()

    dma = pltpu.SemaphoreType.DMA
    return pl.pallas_call(
        kernel,
        out_shape=[jax.ShapeDtypeStruct(part.shape, BF), jax.ShapeDtypeStruct((one, cu), BF),
                   jax.ShapeDtypeStruct((one, cd), BF), jax.ShapeDtypeStruct((nd, nchip, rp, rl), F32)],
        in_specs=[ANY] * 4, out_specs=[ANY] * 4,
        scratch_shapes=[
            pltpu.VMEM((4, two, cu), BF), pltpu.VMEM((4, two, cd), BF),
            pltpu.VMEM((one, cu), F32), pltpu.VMEM((one, cd), F32),
            pltpu.VMEM((one, cu), BF), pltpu.VMEM((one, cd), BF),
            pltpu.VMEM((one, cu), BF), pltpu.VMEM((one, cd), BF),
            pltpu.VMEM((nd, rp, rc), F32), pltpu.VMEM((rp, rc), F32), pltpu.VMEM((rp, rc), F32),
            pltpu.VMEM((nchip, rp, rl), F32), pltpu.VMEM((nchip, rp, rl), F32), pltpu.VMEM((nchip, rp, rl), F32),
            dma((1,)), dma((1,)), dma((1,)), dma((3, 2)), dma((3, 2)), dma((4,)), dma((2,)), dma((2,)),
            dma((5,)), dma((5,)), dma((2,))],
        compiler_params=pltpu.CompilerParams(collective_id=collective_id, has_side_effects=True,
                                             vmem_limit_bytes=48 * 1024 * 1024),
    )(part, grad_up, grad_down, router)


def local(tokens, out_grad, saved_pre, router_weight, slot_expert, slot_of, slot_weight):
    ne = lax.axis_size("expert")
    nd = lax.axis_size("dp")
    rows, width = tokens.shape
    top = slot_of.shape[1]
    half = saved_pre.shape[2] // 2
    experts = router_weight.shape[1]
    slots = slot_expert.shape[0]
    per = rows * top // ne
    total = rows * top

    group = slot_of // nd
    named = group[:, :, None] == jnp.arange(ne, dtype=jnp.int32)[None, None, :]
    names = jnp.sum(named.astype(F32), axis=1)
    before = (lax.broadcasted_iota(jnp.int32, (rows, rows), 1) < lax.broadcasted_iota(jnp.int32, (rows, rows), 0))
    arrival = jnp.dot(before.astype(BF), names.astype(BF), preferred_element_type=F32)
    rank = jnp.sum(jnp.where(named, arrival[:, None, :], 0.0), axis=2).astype(jnp.int32)
    place = (group * per + rank).reshape(-1)
    perm = place[None, :] == lax.broadcasted_iota(jnp.int32, (total, total), 0)
    perm = perm.astype(BF)
    pick = jnp.sum(perm.reshape(total, rows, top).astype(F32), axis=2).astype(BF)

    slot_hot = slot_of[:, :, None] == jnp.arange(slots, dtype=jnp.int32)[None, None, :]
    expert_ids = jnp.sum(jnp.where(slot_hot, slot_expert[None, None, :], 0), axis=2)
    first_expert = jnp.repeat(slot_expert.reshape(ne, nd)[:, 0], nd)
    is_low = jnp.sum(jnp.where(slot_hot, (slot_expert == first_expert).astype(jnp.int32)[None, None, :], 0), axis=2)

    wide_tokens = tokens.astype(F32)
    logits = jnp.dot(wide_tokens, router_weight, precision=lax.Precision.HIGHEST)
    log_total = jax.nn.logsumexp(logits, axis=1)
    router_probs = jnp.exp(logits - log_total[:, None])
    chosen = expert_ids[:, :, None] == jnp.arange(experts, dtype=jnp.int32)[None, None, :]
    chosen_prob = jnp.sum(jnp.where(chosen, router_probs[:, None, :], 0.0), axis=2).astype(BF)
    counts = jnp.sum(chosen.astype(jnp.int32), axis=(0, 1))

    og_send = jnp.dot(pick, out_grad, preferred_element_type=F32).astype(BF).reshape(ne, per, width)
    x_send = jnp.dot(pick, tokens, preferred_element_type=F32).astype(BF).reshape(ne, per, width)
    sv_send = jnp.dot(perm, saved_pre.reshape(total, 2 * half), preferred_element_type=F32).astype(BF)
    sv_send = sv_send.reshape(ne, per, 2 * half)
    facts = jnp.stack([chosen_prob.reshape(-1), is_low.reshape(-1).astype(BF)], axis=1)
    facts = jnp.dot(perm, facts, preferred_element_type=F32).astype(BF).reshape(ne, per, 2)
    facts = jnp.transpose(facts, (0, 2, 1))
    facts = jnp.pad(facts, ((0, 0), (0, 14), (0, 128 - per)))

    og, sv, x, got, both = forward_exchange([og_send, sv_send, x_send, facts], slot_weight[0], ne, nd, 1)
    og, sv, x = og.reshape(total, width), sv.reshape(total, 2 * half), x.reshape(total, width)
    prob = got[:, 0, :per].reshape(total).astype(F32)[:, None]
    low = got[:, 1, :per].reshape(total)[:, None] > 0
    both = both.reshape(2, width, 3 * half)

    gate = sv[:, :half].astype(F32)
    up = sv[:, half:].astype(F32)
    sig = jax.nn.sigmoid(gate)
    active = gate * sig
    hidden = active * up
    back = jnp.where(low, jnp.dot(og, both[0, :, 2 * half:], preferred_element_type=F32),
                     jnp.dot(og, both[1, :, 2 * half:], preferred_element_type=F32))
    prob_grad = jnp.sum(back * hidden, axis=1).astype(BF)
    prob_send = jnp.pad(prob_grad.reshape(ne, 1, per), ((0, 0), (0, 15), (0, 128 - per)))
    (prob_got,) = exchange([prob_send], ne, nd, 2)

    scaled = (prob * hidden).astype(BF)
    hg = prob * back
    pre = jnp.concatenate([hg * up * sig * (1.0 + gate * (1.0 - sig)), hg * active], axis=1).astype(BF)
    zero = jnp.zeros((), BF)
    pre_both = jnp.concatenate([jnp.where(low, pre, zero), jnp.where(low, zero, pre)], axis=1)
    scaled_both = jnp.concatenate([jnp.where(low, scaled, zero), jnp.where(low, zero, scaled)], axis=1)
    contract = (((1,), (1,)), ((), ()))
    part = jnp.where(low, lax.dot_general(pre, both[0, :, :2 * half], contract, preferred_element_type=F32),
                     lax.dot_general(pre, both[1, :, :2 * half], contract, preferred_element_type=F32)).astype(BF)
    grad_up = lax.dot_general(x, pre_both, (((0,), (0,)), ((), ())), preferred_element_type=F32).astype(BF)
    grad_down = lax.dot_general(og, scaled_both, (((0,), (0,)), ((), ())), preferred_element_type=F32).astype(BF)

    prob_row = prob_got[:, 0, :per].reshape(total)
    prob_back = lax.dot_general(perm, prob_row[:, None], (((0,), (0,)), ((), ())), preferred_element_type=F32)
    prob_back = prob_back.reshape(rows, top)
    probs_grad = jnp.sum(jnp.where(chosen, prob_back[:, :, None], 0.0), axis=1)
    probs_grad = probs_grad + balance_coef * experts * counts.astype(F32) / total
    inner = jnp.sum(router_probs * probs_grad, axis=1, keepdims=True)
    logits_grad = router_probs * (probs_grad - inner) + 2.0 * zloss_coef * log_total[:, None] * router_probs
    local_router = lax.dot_general(logits_grad, wide_tokens, (((0,), (0,)), ((), ())),
                                   precision=lax.Precision.HIGHEST)

    part_back, sum_up, sum_down, router_all = backward_exchange(
        part.reshape(ne, per, width), grad_up, grad_down, local_router, ne, nd, 3)
    expert_part = lax.dot_general(pick, part_back.reshape(total, width), (((0,), (0,)), ((), ())),
                                  preferred_element_type=F32)
    router_part = jnp.dot(logits_grad, router_weight.T, precision=lax.Precision.HIGHEST)
    token_grad = (expert_part + router_part).astype(BF)
    router_grad = jnp.transpose(router_all, (0, 2, 1, 3)).reshape(experts, width).T

    low_grad = jnp.concatenate([sum_up[:, :2 * half], sum_down[:, :half]], axis=1)
    high_grad = jnp.concatenate([sum_up[:, 2 * half:], sum_down[:, half:]], axis=1)
    e = lax.axis_index("expert")
    low_first = slot_expert[e * nd] == 2 * e
    expert_grads = jnp.stack([jnp.where(low_first, low_grad, high_grad),
                              jnp.where(low_first, high_grad, low_grad)], axis=1)
    return (token_grad, expert_grads, router_grad)


def solution(mesh):
    placed = (
        P(("expert", "dp"), None),
        P(("expert", "dp"), None),
        P(("expert", "dp"), None, None),
        P(),
        P(),
        P(("expert", "dp"), None),
        P(("expert", "dp"), None, None),
    )
    return jax.shard_map(
        local,
        mesh=mesh,
        in_specs=placed,
        out_specs=(P(("expert", "dp"), None), P("dp", "expert", None), P()),
        check_vma=False,
    )
```

```python
import jax
import jax.numpy as jnp
from jax import lax
from jax.experimental import pallas as pl
from jax.experimental.pallas import tpu as pltpu
from jax.sharding import PartitionSpec as P

zloss_coef = 0.001
balance_coef = 0.01
MESH = pl.DeviceIdType.MESH
ANY = pl.BlockSpec(memory_space=pl.ANY)
BF = jnp.bfloat16
F32 = jnp.float32


def greet(ne, nd, with_expert, with_dp):
    e, d = lax.axis_index("expert"), lax.axis_index("dp")
    barrier = pltpu.get_barrier_semaphore()
    total = 0
    if with_expert:
        def one(i, _):
            pl.semaphore_signal(barrier, inc=1, device_id=(lax.rem(e + i, ne), d), device_id_type=MESH)
            return 0
        lax.fori_loop(1, ne, one, 0)
        total += ne - 1
    if with_dp:
        def two(i, _):
            pl.semaphore_signal(barrier, inc=1, device_id=(e, lax.rem(d + i, nd)), device_id_type=MESH)
            return 0
        lax.fori_loop(1, nd, two, 0)
        total += nd - 1
    pl.semaphore_wait(barrier, total)


def send_all(ne, srcs, dsts, send_sem, recv_sem, local_sem):
    e, d = lax.axis_index("expert"), lax.axis_index("dp")
    for n, (src, dst) in enumerate(zip(srcs, dsts)):
        def one(i, _):
            half = (i + 1) // 2
            odd = lax.rem(i, 2)
            off = odd * half + (1 - odd) * (ne - half)
            peer = lax.rem(e + off, ne)
            pltpu.make_async_remote_copy(
                src_ref=src.at[peer], dst_ref=dst.at[e],
                send_sem=send_sem.at[n], recv_sem=recv_sem.at[n],
                device_id=(peer, d), device_id_type=MESH).start()
            return 0
        lax.fori_loop(1, ne, one, 0)
        pltpu.make_async_copy(src.at[e], dst.at[e], local_sem.at[n]).start()


def wait_all(ne, srcs, dsts, send_sem, recv_sem, local_sem):
    e, d = lax.axis_index("expert"), lax.axis_index("dp")
    for n, (src, dst) in enumerate(zip(srcs, dsts)):
        pltpu.make_async_remote_copy(
            src_ref=src.at[pl.ds(0, ne - 1)], dst_ref=dst.at[pl.ds(0, ne - 1)],
            send_sem=send_sem.at[n], recv_sem=recv_sem.at[n],
            device_id=(lax.rem(e + 1, ne), d), device_id_type=MESH).wait()
        pltpu.make_async_copy(src.at[e], dst.at[e], local_sem.at[n]).wait()


def forward_exchange(tokens, out_grad, saved, facts, pick, weight, ne, nd, collective_id):
    rows, width = tokens.shape
    nz = pick.shape[0]
    nq = ne // nz
    per = saved.shape[1]
    cols = weight.shape[1]
    wr = width // nd
    nc = 3
    cw = cols // nc
    tile = 512
    hops = nz // 2

    def kernel(tok, og, sv, fa, pk, w, og_r, x_r, sv_r, fa_r, both,
               ring, picked, hot,
               in_sem, pk_sem, ring_send, ring_recv, sel_send, sel_recv, sel_local,
               send_sem, recv_sem, local_sem, root_send, piece_sem, y_send, y_recv,
               x_send, x_recv, r_send, r_recv):
        e, d = lax.axis_index("expert"), lax.axis_index("dp")
        core = lax.rem(e, 2)
        z = lax.rem(e // 2, nz)
        hi = e // (2 * nz)
        quarter = hi * 2 + core

        def at(zz):
            return hi * (2 * nz) + zz * 2 + core

        loads = [pltpu.make_async_copy(og, ring.at[0, z], in_sem.at[0]),
                 pltpu.make_async_copy(tok, ring.at[1, z], in_sem.at[1]),
                 pltpu.make_async_copy(pk.at[z], hot.at[z], in_sem.at[2])]
        for c in loads:
            c.start()
        greet(ne, nd, True, True)

        order = (2, 0, 1)
        for side, root in ((0, 0), (1, nd - 1)):
            @pl.when(d == root)
            def _():
                for c in order:
                    span = pl.ds(c * cw, cw)
                    pltpu.make_async_copy(
                        w.at[pl.ds(root * wr, wr), span], both.at[side, root, :, span], piece_sem.at[side, c]).start()
                    for j in [1, 7, 2, 6, 3, 5, 4]:
                        q = (root + j) % nd
                        pltpu.make_async_remote_copy(
                            src_ref=w.at[pl.ds(q * wr, wr), span], dst_ref=both.at[side, q, :, span],
                            send_sem=root_send.at[side], recv_sem=piece_sem.at[side, c],
                            device_id=(e, q), device_id_type=MESH).start()

        def hot_send(i, _):
            q = lax.rem(z + i, nz)
            pltpu.make_async_remote_copy(
                src_ref=pk.at[q], dst_ref=hot.at[z], send_sem=pk_sem.at[0], recv_sem=pk_sem.at[1],
                device_id=(at(q), d), device_id_type=MESH).start()
            return 0
        lax.fori_loop(1, nz, hot_send, 0)

        def ring_copy(n, direction, step):
            sign = 1 - 2 * direction
            block = lax.rem(z - sign * step + nz, nz)
            to = lax.rem(z + sign + nz, nz)
            part = pl.ds(0, rows) if step < hops - 1 else pl.ds(direction * (rows // 2), rows // 2)
            return pltpu.make_async_remote_copy(
                src_ref=ring.at[n, block, part], dst_ref=ring.at[n, block, part],
                send_sem=ring_send.at[n, direction, step], recv_sem=ring_recv.at[n, direction, step],
                device_id=(at(to), d), device_id_type=MESH)

        copies = {(n, g, s): ring_copy(n, g, s) for n in range(2) for g in range(2) for s in range(hops)}
        for n in range(2):
            loads[n].wait()
            for g in range(2):
                copies[n, g, 0].start()
        send_all(ne, [sv, fa], [sv_r, fa_r], send_sem, recv_sem, local_sem)

        loads[2].wait()
        pltpu.make_async_remote_copy(
            src_ref=pk.at[pl.ds(0, nz - 1)], dst_ref=hot.at[pl.ds(0, nz - 1)],
            send_sem=pk_sem.at[0], recv_sem=pk_sem.at[1], device_id=(at(lax.rem(z + 1, nz)), d),
            device_id_type=MESH).wait()
        outs = (og_r, x_r)

        def choose(n, block):
            def one(i, _):
                span = pl.ds(pl.multiple_of(i * tile, tile), tile)
                picked[n, block, :, span] = jnp.dot(
                    hot[block], ring[n, block, :, span], preferred_element_type=F32).astype(BF)
                return 0
            lax.fori_loop(0, width // tile, one, 0)
            src_index = at(block)

            def hand(i, _):
                q = lax.rem(quarter + i, nq)
                pltpu.make_async_remote_copy(
                    src_ref=picked.at[n, block, pl.ds(pl.multiple_of(q * per, per), per)],
                    dst_ref=outs[n].at[src_index], send_sem=sel_send.at[n], recv_sem=sel_recv.at[n],
                    device_id=((q // 2) * (2 * nz) + z * 2 + lax.rem(q, 2), d), device_id_type=MESH).start()
                return 0
            lax.fori_loop(1, nq, hand, 0)
            pltpu.make_async_copy(
                picked.at[n, block, pl.ds(pl.multiple_of(quarter * per, per), per)],
                outs[n].at[src_index], sel_local.at[n]).start()

        pair = d + 1 - 2 * lax.rem(d, 2)
        x, y = d // 2, lax.rem(d, 2)
        nx = nd // 2

        def scattered(c):
            span = pl.ds(c * cw, cw)
            for side in range(2):
                pltpu.make_async_copy(
                    w.at[pl.ds(0, wr), span], both.at[side, d, :, span], piece_sem.at[side, c]).wait()

        def along_y(c):
            part = both.at[pl.ds(0, 2), d, :, pl.ds(c * cw, cw)]
            return pltpu.make_async_remote_copy(
                src_ref=part, dst_ref=part, send_sem=y_send.at[c], recv_sem=y_recv.at[c],
                device_id=(e, pair), device_id_type=MESH)

        def along_x(c, g):
            part = both.at[pl.ds(0, 2), pl.ds(x * 2, 2), :, pl.ds(c * cw, cw)]
            to = lax.rem(x + 1 + 2 * g, nx)
            return pltpu.make_async_remote_copy(
                src_ref=part, dst_ref=part, send_sem=x_send.at[c, g], recv_sem=x_recv.at[c, g],
                device_id=(e, to * 2 + y), device_id_type=MESH)

        def relay(c, g):
            source = lax.rem(x + 3 - 2 * g, nx)
            part = both.at[g, pl.ds(source * 2, 2), :, pl.ds(c * cw, cw)]
            to = lax.rem(x + 1 + 2 * g, nx)
            return pltpu.make_async_remote_copy(
                src_ref=part, dst_ref=part, send_sem=r_send.at[c, g], recv_sem=r_recv.at[c, g],
                device_id=(e, to * 2 + y), device_id_type=MESH)

        ys = {c: along_y(c) for c in order}
        xs = {(c, g): along_x(c, g) for c in order for g in range(2)}
        rs = {(c, g): relay(c, g) for c in order for g in range(2)}

        def stage_y(c):
            scattered(c)
            ys[c].start()

        def stage_x(c):
            ys[c].wait()
            for g in range(2):
                xs[c, g].start()

        def stage_r(c):
            for g in range(2):
                xs[c, g].wait()
                rs[c, g].start()

        def ring_step(s):
            for n in range(2):
                for g in range(2):
                    copies[n, g, s].wait()
                    if s + 1 < hops:
                        copies[n, g, s + 1].start()
            for n in range(2):
                choose(n, lax.rem(z + nz - s - 1, nz))
                if s + 1 < hops:
                    choose(n, lax.rem(z + s + 1, nz))

        for n in range(2):
            choose(n, z)
        stage_y(order[0])
        stage_x(order[0])
        ring_step(0)
        stage_y(order[1])
        stage_x(order[1])
        stage_r(order[0])
        ring_step(1)
        stage_y(order[2])
        stage_x(order[2])
        stage_r(order[1])
        ring_step(2)
        stage_r(order[2])
        ring_step(3)
        for c in order:
            for g in range(2):
                rs[c, g].wait()
        wait_all(ne, [sv, fa], [sv_r, fa_r], send_sem, recv_sem, local_sem)
        for n in range(2):
            far = nz * (nq - 1)
            pltpu.make_async_remote_copy(
                src_ref=outs[n].at[pl.ds(0, far)], dst_ref=outs[n].at[pl.ds(0, far)],
                send_sem=sel_send.at[n], recv_sem=sel_recv.at[n], device_id=(at(lax.rem(z + 1, nz)), d),
                device_id_type=MESH).wait()
            pltpu.make_async_copy(
                outs[n].at[pl.ds(0, nz)], outs[n].at[pl.ds(0, nz)], sel_local.at[n]).wait()
        for side, root in ((0, 0), (1, nd - 1)):
            @pl.when(d == root)
            def _():
                pltpu.make_async_remote_copy(
                    src_ref=both.at[side, pl.ds(0, nd - 1)], dst_ref=both.at[side, pl.ds(0, nd - 1)],
                    send_sem=root_send.at[side], recv_sem=piece_sem.at[side, 0],
                    device_id=(e, (root + 1) % nd), device_id_type=MESH).wait_send()

    dma = pltpu.SemaphoreType.DMA
    shape = jax.ShapeDtypeStruct
    return pl.pallas_call(
        kernel,
        out_shape=[shape((ne, per, width), BF), shape((ne, per, width), BF), shape(saved.shape, BF),
                   shape(facts.shape, BF), shape((2, nd, wr, cols), BF)],
        in_specs=[ANY] * 6, out_specs=[ANY] * 5,
        scratch_shapes=[
            pltpu.VMEM((2, nz, rows, width), BF), pltpu.VMEM((2, nz, rows, width), BF),
            pltpu.VMEM((nz, nq * per, rows), BF),
            dma((3,)), dma((2,)), dma((2, 2, hops)), dma((2, 2, hops)), dma((2,)), dma((2,)), dma((2,)),
            dma((2,)), dma((2,)), dma((2,)), dma((2,)), dma((2, nc)), dma((nc,)), dma((nc,)),
            dma((nc, 2)), dma((nc, 2)), dma((nc, 2)), dma((nc, 2))],
        compiler_params=pltpu.CompilerParams(collective_id=collective_id, has_side_effects=True,
                                             vmem_limit_bytes=40 * 1024 * 1024),
    )(tokens, out_grad, saved, facts, pick, weight)


def backward_exchange(x_rows, og_rows, pre, scaled, both, prob, hot_expert, hot_token, probs, base, extra, tokens,
                      ne, nd, collective_id):
    total, width = x_rows.shape
    per = total // ne
    nx = nd // 2
    two = width // nx
    one = width // nd
    cw = scaled.shape[1]
    rows = tokens.shape[0]
    experts = 2 * ne
    rp = experts // nd
    nchip = ne // 2
    rl = width // nchip
    nc = 3
    st = 32

    def kernel(xr, ogr, pr, sc, wb, qr, he, ht, pb, ba, ex, tk, back, ow, orouter, olg,
               xv, ov, pv, sv, wv, qv, hev, htv, pbv, bav, exv, tkv, lg, partv,
               far, near, own, got_half, got_full, yout, yin,
               rpart, rbuf, racc, rcore, rmine, rpiece, rfull,
               in_sem, q_sem, q_local, send_sem, recv_sem, local_sem,
               a_send, a_recv, b_send, b_recv, y_send, y_recv, r_send, r_recv, misc, fin_sem):
        e, d = lax.axis_index("expert"), lax.axis_index("dp")
        x, y = d // 2, lax.rem(d, 2)
        plus, minus, across = lax.rem(x + 1, nx), lax.rem(x + 3, nx), lax.rem(x + 2, nx)
        pairs = [(ogr, ov), (sc, sv), (xr, xv), (pr, pv), (he, hev), (ht, htv), (pb, pbv), (ba, bav), (ex, exv),
                 (tk, tkv), (wb.at[pl.ds(0, 2), pl.ds(0, nd), :, pl.ds(0, cw)], wv)]
        loads = [pltpu.make_async_copy(s, t, in_sem.at[n]) for n, (s, t) in enumerate(pairs)]
        for c in loads:
            c.start()
        greet(ne, nd, True, True)
        send_all(ne, [qr], [qv], q_sem.at[pl.ds(0, 1)], q_sem.at[pl.ds(1, 1)], q_local)

        def operand(c):
            if c == 0:
                return ov, sv, 0
            return xv, pv, (c - 1) * cw

        def contribute(c, target, out):
            left, right, at = operand(c)

            def half(i, _):
                from_row = pl.multiple_of(target * two + i * one, one)
                out[pl.ds(pl.multiple_of(i * one, one), one), :] = lax.dot_general(
                    left[:, pl.ds(from_row, one)], right[:, pl.ds(at, cw)], (((0,), (0,)), ((), ())),
                    preferred_element_type=F32).astype(BF)
                return 0
            lax.fori_loop(0, 2, half, 0)

        def first(c, g):
            return pltpu.make_async_remote_copy(
                src_ref=far.at[c, pl.ds(g * one, one)], dst_ref=got_half.at[c, g],
                send_sem=a_send.at[c, g], recv_sem=a_recv.at[c, g],
                device_id=(e, (plus if g == 0 else minus) * 2 + y), device_id_type=MESH)

        def second(c, g):
            return pltpu.make_async_remote_copy(
                src_ref=near.at[c, g], dst_ref=got_full.at[c, g],
                send_sem=b_send.at[c, g], recv_sem=b_recv.at[c, g],
                device_id=(e, (plus if g == 0 else minus) * 2 + y), device_id_type=MESH)

        def swap(c):
            return pltpu.make_async_remote_copy(
                src_ref=yout.at[c], dst_ref=yin.at[c], send_sem=y_send.at[c], recv_sem=y_recv.at[c],
                device_id=(e, d + 1 - 2 * y), device_id_type=MESH)

        firsts = {(c, g): first(c, g) for c in range(nc) for g in range(2)}
        seconds = {(c, g): second(c, g) for c in range(nc) for g in range(2)}
        swaps = [swap(c) for c in range(nc)]

        def start_far(c):
            contribute(c, across, far.at[c])
            for g in range(2):
                firsts[c, g].start()

        def start_near(c):
            for g in range(2):
                firsts[c, g].wait()

                def add(i, _):
                    src = pl.ds(pl.multiple_of(i * st, st), st)
                    dst = pl.ds(pl.multiple_of(g * one + i * st, st), st)
                    near[c, g, dst, :] = (near[c, g, dst, :].astype(F32)
                                          + got_half[c, g, src, :].astype(F32)).astype(BF)
                    return 0
                lax.fori_loop(0, one // st, add, 0)
                seconds[c, g].start()

        def start_swap(c):
            for g in range(2):
                seconds[c, g].wait()

            def add(i, _):
                src = pl.ds(pl.multiple_of((1 - y) * one + i * st, st), st)
                yout[c, pl.ds(pl.multiple_of(i * st, st), st), :] = (
                    own[c, src, :].astype(F32) + got_full[c, 0, src, :].astype(F32)
                    + got_full[c, 1, src, :].astype(F32)).astype(BF)
                return 0
            lax.fori_loop(0, one // st, add, 0)
            swaps[c].start()

        def finish(c):
            swaps[c].wait()

            def add(i, _):
                src = pl.ds(pl.multiple_of(y * one + i * st, st), st)
                at = pl.ds(pl.multiple_of(i * st, st), st)
                yout[c, at, :] = (
                    own[c, src, :].astype(F32) + got_full[c, 0, src, :].astype(F32)
                    + got_full[c, 1, src, :].astype(F32) + yin[c, at, :].astype(F32)).astype(BF)
                return 0
            lax.fori_loop(0, one // st, add, 0)
            pltpu.make_async_copy(yout.at[c], ow.at[c], fin_sem.at[c]).start()

        loads[0].wait()
        loads[1].wait()
        start_far(0)
        loads[2].wait()
        loads[3].wait()
        start_far(1)
        start_far(2)

        for n in range(4, 10):
            loads[n].wait()
        wait_all(ne, [qr], [qv], q_sem.at[pl.ds(0, 1)], q_sem.at[pl.ds(1, 1)], q_local)
        chosen = hev[...] * qv[...].reshape(total, 128)
        grad = jnp.dot(htv[...], chosen, preferred_element_type=F32) + bav[...]
        inner = jnp.sum(pbv[...] * grad, axis=1, keepdims=True)
        grad = pbv[...] * (grad - inner) + exv[...]
        lg[...] = grad
        lg_out = pltpu.make_async_copy(lg, olg, misc.at[3])
        lg_out.start()
        turned = grad.T[:experts]
        high = turned.astype(BF)
        rest = turned - high.astype(F32)
        middle = rest.astype(BF)
        low = (rest - middle.astype(F32)).astype(BF)

        def router_tile(i, _):
            span = pl.ds(pl.multiple_of(i * 512, 512), 512)
            t = tkv[:, span]
            rpart[:, span] = (jnp.dot(low, t, preferred_element_type=F32)
                              + jnp.dot(middle, t, preferred_element_type=F32)
                              + jnp.dot(high, t, preferred_element_type=F32))
            return 0
        lax.fori_loop(0, width // 512, router_tile, 0)

        def rs_dp(i, _):
            q = lax.rem(d + i, nd)
            pltpu.make_async_remote_copy(
                src_ref=rpart.at[pl.ds(pl.multiple_of(q * rp, rp), rp)], dst_ref=rbuf.at[d],
                send_sem=r_send.at[0], recv_sem=r_recv.at[0], device_id=(e, q), device_id_type=MESH).start()
            return 0
        lax.fori_loop(1, nd, rs_dp, 0)
        rbuf[d] = rpart[pl.ds(pl.multiple_of(d * rp, rp), rp), :]

        contribute(0, plus, near.at[0, 0])
        contribute(0, minus, near.at[0, 1])

        pltpu.make_async_remote_copy(
            src_ref=rbuf.at[pl.ds(0, nd - 1)], dst_ref=rbuf.at[pl.ds(0, nd - 1)],
            send_sem=r_send.at[0], recv_sem=r_recv.at[0], device_id=(e, lax.rem(d + 1, nd)),
            device_id_type=MESH).wait()
        racc[...] = jnp.sum(rbuf[...], axis=0)
        mate = e + 1 - 2 * lax.rem(e, 2)
        core = lax.rem(e, 2)
        chip = e // 2
        cc = pltpu.make_async_remote_copy(
            src_ref=racc, dst_ref=rcore, send_sem=r_send.at[1], recv_sem=r_recv.at[1],
            device_id=(mate, d), device_id_type=MESH)
        cc.start()

        start_near(0)
        contribute(1, plus, near.at[1, 0])
        contribute(1, minus, near.at[1, 1])

        cc.wait()
        for n in range(nchip):
            rmine[n] = racc[:, n * rl:(n + 1) * rl] + rcore[:, n * rl:(n + 1) * rl]

        def rs_chip(i, _):
            q = lax.rem(chip + i, nchip)
            pltpu.make_async_remote_copy(
                src_ref=rmine.at[q], dst_ref=rpiece.at[chip], send_sem=r_send.at[2], recv_sem=r_recv.at[2],
                device_id=(q * 2 + core, d), device_id_type=MESH).start()
            return 0
        lax.fori_loop(1, nchip, rs_chip, 0)
        rpiece[chip] = rmine[chip]

        loads[10].wait()

        def part_tile(i, _):
            j, r = i // 4, lax.rem(i, 4)
            at = pl.ds(pl.multiple_of(r * (total // 4), total // 4), total // 4)
            contract = (((1,), (1,)), ((), ()))
            value = lax.dot_general(pv[at, :cw], wv[0, j], contract, preferred_element_type=F32)
            value = value + lax.dot_general(pv[at, cw:], wv[1, j], contract, preferred_element_type=F32)
            span = pl.ds(pl.multiple_of(j * one, one), one)
            partv[pl.ds(r * (ne // 4), ne // 4), :, span] = value.astype(BF).reshape(ne // 4, per, one)
            return 0
        lax.fori_loop(0, 4 * nd, part_tile, 0)
        send_all(ne, [partv], [back], send_sem, recv_sem, local_sem)

        start_near(1)
        pltpu.make_async_remote_copy(
            src_ref=rpiece.at[pl.ds(0, nchip - 1)], dst_ref=rpiece.at[pl.ds(0, nchip - 1)],
            send_sem=r_send.at[2], recv_sem=r_recv.at[2], device_id=(mate, d), device_id_type=MESH).wait()
        rfull[chip] = jnp.sum(rpiece[...], axis=0)

        def ag_chip(i, _):
            q = lax.rem(chip + i, nchip)
            pltpu.make_async_remote_copy(
                src_ref=rfull.at[chip], dst_ref=rfull.at[chip], send_sem=r_send.at[3], recv_sem=r_recv.at[3],
                device_id=(q * 2 + core, d), device_id_type=MESH).start()
            return 0
        lax.fori_loop(1, nchip, ag_chip, 0)

        contribute(2, plus, near.at[2, 0])
        contribute(2, minus, near.at[2, 1])
        start_near(2)
        for c in range(nc):
            contribute(c, x, own.at[c])

        pltpu.make_async_remote_copy(
            src_ref=rfull.at[pl.ds(0, nchip - 1)], dst_ref=rfull.at[pl.ds(0, nchip - 1)],
            send_sem=r_send.at[3], recv_sem=r_recv.at[3], device_id=(mate, d), device_id_type=MESH).wait()

        def ag_dp(i, _):
            q = lax.rem(d + i, nd)
            pltpu.make_async_remote_copy(
                src_ref=rfull, dst_ref=orouter.at[d], send_sem=r_send.at[4], recv_sem=r_recv.at[4],
                device_id=(e, q), device_id_type=MESH).start()
            return 0
        lax.fori_loop(1, nd, ag_dp, 0)
        own_f = pltpu.make_async_copy(rfull, orouter.at[d], misc.at[0])
        own_f.start()

        start_swap(0)
        start_swap(1)
        finish(0)
        start_swap(2)
        finish(1)
        finish(2)

        pltpu.make_async_remote_copy(
            src_ref=orouter.at[pl.ds(0, nd - 1)], dst_ref=orouter.at[pl.ds(0, nd - 1)],
            send_sem=r_send.at[4], recv_sem=r_recv.at[4], device_id=(e, lax.rem(d + 1, nd)),
            device_id_type=MESH).wait()
        own_f.wait()
        lg_out.wait()
        wait_all(ne, [partv], [back], send_sem, recv_sem, local_sem)
        for c in range(nc):
            pltpu.make_async_copy(yout.at[c], ow.at[c], fin_sem.at[c]).wait()

    dma = pltpu.SemaphoreType.DMA
    shape = jax.ShapeDtypeStruct
    vmem = pltpu.VMEM
    return pl.pallas_call(
        kernel,
        out_shape=[shape((ne, per, width), BF), shape((nc, one, cw), BF), shape((nd, nchip, rp, rl), F32),
                   shape((rows, 128), F32)],
        in_specs=[ANY] * 12, out_specs=[ANY] * 4,
        scratch_shapes=[
            vmem((total, width), BF), vmem((total, width), BF), vmem((total, 2 * cw), BF), vmem((total, cw), BF),
            vmem((2, nd, one, cw), BF), vmem((ne, per, 128), BF), vmem((total, 128), BF), vmem((rows, total), BF),
            vmem((rows, 128), F32), vmem((1, 128), F32), vmem((rows, 128), F32), vmem((rows, width), BF),
            vmem((rows, 128), F32), vmem((ne, per, width), BF),
            vmem((nc, two, cw), BF), vmem((nc, 2, two, cw), BF), vmem((nc, two, cw), BF),
            vmem((nc, 2, one, cw), BF), vmem((nc, 2, two, cw), BF), vmem((nc, one, cw), BF), vmem((nc, one, cw), BF),
            vmem((experts, width), F32), vmem((nd, rp, width), F32), vmem((rp, width), F32), vmem((rp, width), F32),
            vmem((nchip, rp, rl), F32), vmem((nchip, rp, rl), F32), vmem((nchip, rp, rl), F32),
            dma((11,)), dma((2,)), dma((1,)), dma((1,)), dma((1,)), dma((1,)),
            dma((nc, 2)), dma((nc, 2)), dma((nc, 2)), dma((nc, 2)), dma((nc,)), dma((nc,)),
            dma((5,)), dma((5,)), dma((4,)), dma((nc,))],
        compiler_params=pltpu.CompilerParams(collective_id=collective_id, has_side_effects=True,
                                             vmem_limit_bytes=60 * 1024 * 1024),
    )(x_rows, og_rows, pre, scaled, both, prob, hot_expert, hot_token, probs, base, extra, tokens)


def local(tokens, out_grad, saved_pre, router_weight, slot_expert, slot_of, slot_weight):
    ne = lax.axis_size("expert")
    nd = lax.axis_size("dp")
    rows, width = tokens.shape
    top = slot_of.shape[1]
    half = saved_pre.shape[2] // 2
    experts = router_weight.shape[1]
    slots = slot_expert.shape[0]
    per = rows * top // ne
    total = rows * top

    group = slot_of // nd
    named = group[:, :, None] == jnp.arange(ne, dtype=jnp.int32)[None, None, :]
    names = jnp.sum(named.astype(F32), axis=1)
    before = (lax.broadcasted_iota(jnp.int32, (rows, rows), 1) < lax.broadcasted_iota(jnp.int32, (rows, rows), 0))
    arrival = jnp.dot(before.astype(BF), names.astype(BF), preferred_element_type=F32)
    rank = jnp.sum(jnp.where(named, arrival[:, None, :], 0.0), axis=2).astype(jnp.int32)
    place = (group * per + rank).reshape(-1)
    perm = place[None, :] == lax.broadcasted_iota(jnp.int32, (total, total), 0)
    perm = perm.astype(BF)
    pick = jnp.sum(perm.reshape(total, rows, top).astype(F32), axis=2).astype(BF)

    slot_hot = slot_of[:, :, None] == jnp.arange(slots, dtype=jnp.int32)[None, None, :]
    expert_ids = jnp.sum(jnp.where(slot_hot, slot_expert[None, None, :], 0), axis=2)
    first_expert = jnp.repeat(slot_expert.reshape(ne, nd)[:, 0], nd)
    is_low = jnp.sum(jnp.where(slot_hot, (slot_expert == first_expert).astype(jnp.int32)[None, None, :], 0), axis=2)

    wide_tokens = tokens.astype(F32)
    logits = jnp.dot(wide_tokens, router_weight, precision=lax.Precision.HIGHEST)
    log_total = jax.nn.logsumexp(logits, axis=1)
    router_probs = jnp.exp(logits - log_total[:, None])
    chosen = expert_ids[:, :, None] == jnp.arange(experts, dtype=jnp.int32)[None, None, :]
    chosen_prob = jnp.sum(jnp.where(chosen, router_probs[:, None, :], 0.0), axis=2).astype(BF)
    counts = jnp.sum(chosen.astype(jnp.int32), axis=(0, 1))

    hot = pick.reshape(2, ne // 4, 2, per, rows).transpose(1, 0, 2, 3, 4).reshape(ne // 4, 4 * per, rows)
    sv_send = jnp.dot(perm, saved_pre.reshape(total, 2 * half), preferred_element_type=F32).astype(BF)
    sv_send = sv_send.reshape(ne, per, 2 * half)
    facts = jnp.stack([chosen_prob.reshape(-1), is_low.reshape(-1).astype(BF)], axis=1)
    facts = jnp.dot(perm, facts, preferred_element_type=F32).astype(BF).reshape(ne, per, 2)
    facts = jnp.transpose(facts, (0, 2, 1))
    facts = jnp.pad(facts, ((0, 0), (0, 14), (0, 128 - per)))

    og, x, sv, got, both = forward_exchange(tokens, out_grad, sv_send, facts, hot, slot_weight[0], ne, nd, 1)
    og, sv, x = og.reshape(total, width), sv.reshape(total, 2 * half), x.reshape(total, width)
    prob = got[:, 0, :per].reshape(total).astype(F32)[:, None]
    low = got[:, 1, :per].reshape(total)[:, None] > 0
    down = both[:, :, :, 2 * half:].reshape(2, width, half)

    gate = sv[:, :half].astype(F32)
    up = sv[:, half:].astype(F32)
    sig = jax.nn.sigmoid(gate)
    active = gate * sig
    hidden = active * up
    back = jnp.where(low, jnp.dot(og, down[0], preferred_element_type=F32),
                     jnp.dot(og, down[1], preferred_element_type=F32))
    prob_grad = jnp.sum(back * hidden, axis=1).astype(BF)
    prob_send = jnp.broadcast_to(prob_grad[:, None], (total, 128)).reshape(ne, per, 128)

    scaled = (prob * hidden).astype(BF)
    hg = prob * back
    pre = jnp.concatenate([hg * up * sig * (1.0 + gate * (1.0 - sig)), hg * active], axis=1).astype(BF)
    zero = jnp.zeros((), BF)
    pre_both = jnp.concatenate([jnp.where(low, pre, zero), jnp.where(low, zero, pre)], axis=1)
    scaled_both = jnp.concatenate([jnp.where(low, scaled, zero), jnp.where(low, zero, scaled)], axis=1)

    hot_expert = jnp.dot(perm, chosen.reshape(total, experts).astype(BF), preferred_element_type=F32).astype(BF)
    wide = ((0, 0), (0, 128 - experts))
    base = (balance_coef * experts * counts.astype(F32) / total)[None, :]
    extra = 2.0 * zloss_coef * log_total[:, None] * router_probs
    part_back, sums, router_all, logits_grad = backward_exchange(
        x, og, pre_both, scaled_both, both, prob_send, jnp.pad(hot_expert, wide), pick.T, jnp.pad(router_probs, wide),
        jnp.pad(base, wide), jnp.pad(extra, wide), tokens, ne, nd, 3)
    logits_grad = logits_grad[:, :experts]
    expert_part = lax.dot_general(pick, part_back.reshape(total, width), (((0,), (0,)), ((), ())),
                                  preferred_element_type=F32)
    router_part = jnp.dot(logits_grad, router_weight.T, precision=lax.Precision.HIGHEST)
    token_grad = (expert_part + router_part).astype(BF)
    router_grad = jnp.transpose(router_all, (0, 2, 1, 3)).reshape(experts, width).T

    low_grad = jnp.concatenate([sums[1], sums[0, :, :half]], axis=1)
    high_grad = jnp.concatenate([sums[2], sums[0, :, half:]], axis=1)
    e = lax.axis_index("expert")
    low_first = slot_expert[e * nd] == 2 * e
    expert_grads = jnp.stack([jnp.where(low_first, low_grad, high_grad),
                              jnp.where(low_first, high_grad, low_grad)], axis=1)
    return (token_grad, expert_grads, router_grad)


def solution(mesh):
    placed = (
        P(("expert", "dp"), None),
        P(("expert", "dp"), None),
        P(("expert", "dp"), None, None),
        P(),
        P(),
        P(("expert", "dp"), None),
        P(("expert", "dp"), None, None),
    )
    return jax.shard_map(
        local,
        mesh=mesh,
        in_specs=placed,
        out_specs=(P(("expert", "dp"), None), P("dp", "expert", None), P()),
        check_vma=False,
    )
```

```python
import jax
import jax.numpy as jnp
from jax import lax
from jax.experimental import pallas as pl
from jax.experimental.pallas import tpu as pltpu
from jax.sharding import PartitionSpec as P

zloss_coef = 0.001
balance_coef = 0.01
MESH = pl.DeviceIdType.MESH
ANY = pl.BlockSpec(memory_space=pl.ANY)
BF = jnp.bfloat16
F32 = jnp.float32


def greet(ne, nd, with_expert, with_dp):
    e, d = lax.axis_index("expert"), lax.axis_index("dp")
    barrier = pltpu.get_barrier_semaphore()
    total = 0
    if with_expert:
        def one(i, _):
            pl.semaphore_signal(barrier, inc=1, device_id=(lax.rem(e + i, ne), d), device_id_type=MESH)
            return 0
        lax.fori_loop(1, ne, one, 0)
        total += ne - 1
    if with_dp:
        def two(i, _):
            pl.semaphore_signal(barrier, inc=1, device_id=(e, lax.rem(d + i, nd)), device_id_type=MESH)
            return 0
        lax.fori_loop(1, nd, two, 0)
        total += nd - 1
    pl.semaphore_wait(barrier, total)


def send_all(ne, srcs, dsts, send_sem, recv_sem, local_sem, first=1, last=None):
    e, d = lax.axis_index("expert"), lax.axis_index("dp")
    for n, (src, dst) in enumerate(zip(srcs, dsts)):
        def one(i, _):
            half = (i + 1) // 2
            odd = lax.rem(i, 2)
            off = odd * half + (1 - odd) * (ne - half)
            peer = lax.rem(e + off, ne)
            pltpu.make_async_remote_copy(
                src_ref=src.at[peer], dst_ref=dst.at[e],
                send_sem=send_sem.at[n], recv_sem=recv_sem.at[n],
                device_id=(peer, d), device_id_type=MESH).start()
            return 0
        lax.fori_loop(first, ne if last is None else last, one, 0)
        if first == 1:
            pltpu.make_async_copy(src.at[e], dst.at[e], local_sem.at[n]).start()


def wait_all(ne, srcs, dsts, send_sem, recv_sem, local_sem):
    e, d = lax.axis_index("expert"), lax.axis_index("dp")
    for n, (src, dst) in enumerate(zip(srcs, dsts)):
        pltpu.make_async_remote_copy(
            src_ref=src.at[pl.ds(0, ne - 1)], dst_ref=dst.at[pl.ds(0, ne - 1)],
            send_sem=send_sem.at[n], recv_sem=recv_sem.at[n],
            device_id=(lax.rem(e + 1, ne), d), device_id_type=MESH).wait()
        pltpu.make_async_copy(src.at[e], dst.at[e], local_sem.at[n]).wait()


def fused(tokens, out_grad, saved, facts, pick, weight, hot_expert, hot_token, probs, base, extra, ne, nd):
    rows, width = tokens.shape
    nz = pick.shape[0]
    nq = ne // nz
    per = saved.shape[1]
    half = saved.shape[2] // 2
    total = ne * per
    cols = weight.shape[1]
    wr = width // nd
    nc = 3
    cw = cols // nc
    gw = 2 * cw
    tile = 512
    hops = nz // 2
    nx = nd // 2
    two = width // nx
    one = width // nd
    experts = 2 * ne
    rp = experts // nd
    nchip = ne // 2
    rl = width // nchip
    st = 32
    slots = 4

    def kernel(tok, og, sv, fa, pk, w, he, ht, pb, ba, ex, both, back, ow, orouter, olg,
               ring, picked, hot, ov, xv, svv, fav, wv, pv, cv, qs, qv, hev, htv, pbv, bav, exv, tkv, lg,
               far, near, got_half, got_full, yout, yin,
               rpart, rbuf, racc, rcore, rmine, rpiece, rfull,
               in_sem, pk_sem, ring_send, ring_recv, sel_send, sel_recv, sel_local,
               send_sem, recv_sem, local_sem, root_send, piece_sem, y_send, y_recv,
               x_send, x_recv, r_send, r_recv,
               q_sem, q_local, p_send, p_recv, p_local, a_send, a_recv, b_send, b_recv, s_send, s_recv,
               t_send, t_recv, misc, fin_sem):
        e, d = lax.axis_index("expert"), lax.axis_index("dp")
        core = lax.rem(e, 2)
        z = lax.rem(e // 2, nz)
        hi = e // (2 * nz)
        quarter = hi * 2 + core

        def at(zz):
            return hi * (2 * nz) + zz * 2 + core

        loads = [pltpu.make_async_copy(og, ring.at[0, z], in_sem.at[0]),
                 pltpu.make_async_copy(tok, ring.at[1, z], in_sem.at[1]),
                 pltpu.make_async_copy(pk.at[z], hot.at[z], in_sem.at[2])]
        facts_in = [pltpu.make_async_copy(s, t, in_sem.at[3 + n]) for n, (s, t) in enumerate(
            ((he, hev), (ht, htv), (pb, pbv), (ba, bav), (ex, exv), (tok, tkv)))]
        for c in loads + facts_in:
            c.start()
        greet(ne, nd, True, True)

        order = (2, 0, 1)
        for side, root in ((0, 0), (1, nd - 1)):
            @pl.when(d == root)
            def _():
                for c in order:
                    span = pl.ds(c * cw, cw)
                    mine = (root // 2) * 2
                    pltpu.make_async_copy(
                        w.at[pl.ds(mine * wr, 2 * wr), span], both.at[side, root // 2, :, span],
                        piece_sem.at[side, c]).start()
                    for j in (1, 3, 2):
                        q = (root // 2 + j) % (nd // 2)
                        pltpu.make_async_remote_copy(
                            src_ref=w.at[pl.ds(q * 2 * wr, 2 * wr), span], dst_ref=both.at[side, q, :, span],
                            send_sem=root_send.at[side], recv_sem=piece_sem.at[side, c],
                            device_id=(e, q * 2 + root % 2), device_id_type=MESH).start()

        def hot_send(i, _):
            q = lax.rem(z + i, nz)
            pltpu.make_async_remote_copy(
                src_ref=pk.at[q], dst_ref=hot.at[z], send_sem=pk_sem.at[0], recv_sem=pk_sem.at[1],
                device_id=(at(q), d), device_id_type=MESH).start()
            return 0
        lax.fori_loop(1, nz, hot_send, 0)

        def ring_copy(n, direction, step):
            sign = 1 - 2 * direction
            block = lax.rem(z - sign * step + nz, nz)
            to = lax.rem(z + sign + nz, nz)
            part = pl.ds(0, rows) if step < hops - 1 else pl.ds(direction * (rows // 2), rows // 2)
            return pltpu.make_async_remote_copy(
                src_ref=ring.at[n, block, part], dst_ref=ring.at[n, block, part],
                send_sem=ring_send.at[n, direction, step], recv_sem=ring_recv.at[n, direction, step],
                device_id=(at(to), d), device_id_type=MESH)

        copies = {(n, g, s): ring_copy(n, g, s) for n in range(2) for g in range(2) for s in range(hops)}

        def rows_out(first, last):
            send_all(ne, [sv, fa], [svv, fav], send_sem, recv_sem, local_sem, first, last)

        def hot_wait():
            loads[2].wait()
            pltpu.make_async_remote_copy(
                src_ref=pk.at[pl.ds(0, nz - 1)], dst_ref=hot.at[pl.ds(0, nz - 1)],
                send_sem=pk_sem.at[0], recv_sem=pk_sem.at[1], device_id=(at(lax.rem(z + 1, nz)), d),
                device_id_type=MESH).wait()

        outs = (ov, xv)
        uses = [0, 0]

        def drain(n, slot):
            some = pl.ds(0, (nq - 1) * per)
            pltpu.make_async_remote_copy(
                src_ref=picked.at[n, slot, some], dst_ref=picked.at[n, slot, some],
                send_sem=sel_send.at[n, slot], recv_sem=sel_recv.at[n], device_id=(at(lax.rem(z + 1, nz)), d),
                device_id_type=MESH).wait_send()
            pltpu.make_async_copy(picked.at[n, slot, pl.ds(0, per)], outs[n].at[0], sel_local.at[n, slot]).wait()

        def choose(n, block):
            slot = uses[n] % slots
            if uses[n] >= slots:
                drain(n, slot)
            uses[n] += 1

            def pick_tile(i, _):
                span = pl.ds(pl.multiple_of(i * tile, tile), tile)
                picked[n, slot, :, span] = jnp.dot(
                    hot[block], ring[n, block, :, span], preferred_element_type=F32).astype(BF)
                return 0
            lax.fori_loop(0, width // tile, pick_tile, 0)
            src_index = at(block)

            def hand(i, _):
                q = lax.rem(quarter + i, nq)
                pltpu.make_async_remote_copy(
                    src_ref=picked.at[n, slot, pl.ds(pl.multiple_of(q * per, per), per)],
                    dst_ref=outs[n].at[src_index], send_sem=sel_send.at[n, slot], recv_sem=sel_recv.at[n],
                    device_id=((q // 2) * (2 * nz) + z * 2 + lax.rem(q, 2), d), device_id_type=MESH).start()
                return 0
            lax.fori_loop(1, nq, hand, 0)
            pltpu.make_async_copy(
                picked.at[n, slot, pl.ds(pl.multiple_of(quarter * per, per), per)],
                outs[n].at[src_index], sel_local.at[n, slot]).start()

        def rows_in(n):
            for slot in range(slots):
                drain(n, slot)
            far_rows = nz * (nq - 1)
            pltpu.make_async_remote_copy(
                src_ref=outs[n].at[pl.ds(0, far_rows)], dst_ref=outs[n].at[pl.ds(0, far_rows)],
                send_sem=sel_send.at[n, 0], recv_sem=sel_recv.at[n], device_id=(at(lax.rem(z + 1, nz)), d),
                device_id_type=MESH).wait_recv()

        pair = d + 1 - 2 * lax.rem(d, 2)
        x, y = d // 2, lax.rem(d, 2)
        nx = nd // 2

        def scattered(c):
            span = pl.ds(c * cw, cw)
            for side in range(2):
                @pl.when(y == side)
                def _():
                    pltpu.make_async_copy(
                        w.at[pl.ds(0, 2 * wr), span], both.at[side, x, :, span], piece_sem.at[side, c]).wait()

        def along_y(c):
            part = both.at[y, x, :, pl.ds(c * cw, cw)]
            return pltpu.make_async_remote_copy(
                src_ref=part, dst_ref=part, send_sem=y_send.at[c], recv_sem=y_recv.at[c],
                device_id=(e, pair), device_id_type=MESH)

        def along_x(c, g):
            part = both.at[pl.ds(0, 2), x, :, pl.ds(c * cw, cw)]
            to = lax.rem(x + 1 + 2 * g, nx)
            return pltpu.make_async_remote_copy(
                src_ref=part, dst_ref=part, send_sem=x_send.at[c, g], recv_sem=x_recv.at[c, g],
                device_id=(e, to * 2 + y), device_id_type=MESH)

        def relay(c, g):
            source = lax.rem(x + 3 - 2 * g, nx)
            part = both.at[g, source, :, pl.ds(c * cw, cw)]
            to = lax.rem(x + 1 + 2 * g, nx)
            return pltpu.make_async_remote_copy(
                src_ref=part, dst_ref=part, send_sem=r_send.at[c, g], recv_sem=r_recv.at[c, g],
                device_id=(e, to * 2 + y), device_id_type=MESH)

        ys = {c: along_y(c) for c in order}
        xs = {(c, g): along_x(c, g) for c in order for g in range(2)}
        rs = {(c, g): relay(c, g) for c in order for g in range(2)}

        def stage_y(c):
            scattered(c)
            ys[c].start()

        def stage_x(c):
            ys[c].wait()
            for g in range(2):
                xs[c, g].start()

        def stage_r(c):
            for g in range(2):
                xs[c, g].wait()
                rs[c, g].start()

        def portion(n):
            rows_out(max(1, n * ne // 4), (n + 1) * ne // 4)

        def ring_start(n):
            loads[n].wait()
            for g in range(2):
                copies[n, g, 0].start()

        def ring_step(n, s):
            for g in range(2):
                copies[n, g, s].wait()
                if s + 1 < hops:
                    copies[n, g, s + 1].start()
            if n == 0 and s < 3:
                portion(s + 1)
            choose(n, lax.rem(z + nz - s - 1, nz))
            if s + 1 < hops:
                choose(n, lax.rem(z + s + 1, nz))

        def relayed(c):
            for g in range(2):
                rs[c, g].wait()

        def down_in():
            relayed(2)
            c = pltpu.make_async_copy(both.at[pl.ds(0, 2), pl.ds(0, nx), :, pl.ds(2 * cw, cw)],
                                      wv.at[pl.ds(0, 2), pl.ds(0, nx), :, pl.ds(0, cw)], misc.at[1])
            c.start()
            c.wait()

        gate_in = pltpu.make_async_copy(both.at[pl.ds(0, 2), pl.ds(0, nx), :, pl.ds(0, gw)], wv, misc.at[2])

        def experts_back():
            wait_all(ne, [sv, fa], [svv, fav], send_sem, recv_sem, local_sem)
            nb = ne // 4

            def block(r, _):
                src = pl.ds(r * nb, nb)
                m = nb * per
                both_back = []
                for side in range(2):
                    value = jnp.zeros((m, half), F32)
                    for j in range(nx):
                        value = value + jnp.dot(ov[src, :, j * two:(j + 1) * two].reshape(m, two),
                                                wv[side, j, :, :half], preferred_element_type=F32)
                    both_back.append(value)
                info = fav[src].reshape(m, 128).astype(F32)
                prob, low = info[:, 0:1], info[:, 1:2]
                gradient = jnp.where(low > 0.5, both_back[0], both_back[1])
                saved_rows = svv[src].reshape(m, 2 * half).astype(F32)
                gate, up = saved_rows[:, :half], saved_rows[:, half:]
                sig = 1.0 / (1.0 + jnp.exp(-gate))
                active = gate * sig
                hidden = active * up
                q = jnp.sum(gradient * hidden, axis=1, keepdims=True)
                qs[src] = jnp.broadcast_to(q, (m, 128)).astype(BF).reshape(nb, per, 128)
                scaled = prob * hidden
                grad = prob * gradient
                gate_grad = grad * up * sig * (1.0 + gate * (1.0 - sig))
                up_grad = grad * active
                at_rows = pl.ds(pl.multiple_of(r * m, m), m)
                is_low = low > 0.5
                cv[at_rows, :half] = jnp.where(is_low, scaled, 0.0).astype(BF)
                cv[at_rows, half:] = jnp.where(is_low, 0.0, scaled).astype(BF)
                pv[at_rows, :half] = jnp.where(is_low, gate_grad, 0.0).astype(BF)
                pv[at_rows, half:2 * half] = jnp.where(is_low, up_grad, 0.0).astype(BF)
                pv[at_rows, 2 * half:3 * half] = jnp.where(is_low, 0.0, gate_grad).astype(BF)
                pv[at_rows, 3 * half:] = jnp.where(is_low, 0.0, up_grad).astype(BF)
                return 0
            lax.fori_loop(0, 4, block, 0)
            send_all(ne, [qs], [qv], q_sem.at[pl.ds(0, 1)], q_sem.at[pl.ds(1, 1)], q_local)

        plus, minus, across = lax.rem(x + 1, nx), lax.rem(x + 3, nx), lax.rem(x + 2, nx)

        def product(c, from_row, n):
            left, right, first_col = (ov, cv, 0) if c == 0 else (xv, pv, (c - 1) * gw)
            return lax.dot_general(
                left[:, :, pl.ds(from_row, n)].reshape(total, n), right[:, pl.ds(first_col, gw)],
                (((0,), (0,)), ((), ())), preferred_element_type=F32)

        def contribute(c, target, out):
            def piece(i, _):
                out[pl.ds(pl.multiple_of(i * one, one), one), :] = product(
                    c, pl.multiple_of(target * two + i * one, one), one).astype(BF)
                return 0
            lax.fori_loop(0, 2, piece, 0)

        def first(c, g):
            return pltpu.make_async_remote_copy(
                src_ref=far.at[c, pl.ds(g * one, one)], dst_ref=got_half.at[c, g],
                send_sem=a_send.at[c, g], recv_sem=a_recv.at[c, g],
                device_id=(e, (plus if g == 0 else minus) * 2 + y), device_id_type=MESH)

        def second(c, g):
            return pltpu.make_async_remote_copy(
                src_ref=near.at[c, g], dst_ref=got_full.at[c, g],
                send_sem=b_send.at[c, g], recv_sem=b_recv.at[c, g],
                device_id=(e, (plus if g == 0 else minus) * 2 + y), device_id_type=MESH)

        def swap(c):
            return pltpu.make_async_remote_copy(
                src_ref=yout.at[c], dst_ref=yin.at[c], send_sem=s_send.at[c], recv_sem=s_recv.at[c],
                device_id=(e, d + 1 - 2 * y), device_id_type=MESH)

        firsts = {(c, g): first(c, g) for c in range(nc) for g in range(2)}
        seconds = {(c, g): second(c, g) for c in range(nc) for g in range(2)}
        swaps = [swap(c) for c in range(nc)]

        def start_near(c):
            for g in range(2):
                firsts[c, g].wait()

                def add(i, _):
                    src = pl.ds(pl.multiple_of(i * st, st), st)
                    dst = pl.ds(pl.multiple_of(g * one + i * st, st), st)
                    near[c, g, dst, :] = (near[c, g, dst, :].astype(F32)
                                          + got_half[c, g, src, :].astype(F32)).astype(BF)
                    return 0
                lax.fori_loop(0, one // st, add, 0)
                seconds[c, g].start()

        def summed(c, side, finish):
            def add(i, _):
                src = pl.ds(pl.multiple_of(side * one + i * 128, 128), 128)
                into = pl.ds(pl.multiple_of(i * 128, 128), 128)
                value = product(c, pl.multiple_of(x * two + side * one + i * 128, 128), 128)
                value = value + got_full[c, 0, src, :].astype(F32) + got_full[c, 1, src, :].astype(F32)
                if finish:
                    value = value + yin[c, into, :].astype(F32)
                yout[c, into, :] = value.astype(BF)
                return 0
            lax.fori_loop(0, one // 128, add, 0)

        def start_swap(c):
            for g in range(2):
                seconds[c, g].wait()
            summed(c, 1 - y, False)
            swaps[c].start()

        def finish(c):
            swaps[c].wait()
            summed(c, y, True)
            pltpu.make_async_copy(yout.at[c], ow.at[c], fin_sem.at[c]).start()

        def start_far(c):
            contribute(c, across, far.at[c])
            for g in range(2):
                firsts[c, g].start()

        def near_both(c):
            contribute(c, plus, near.at[c, 0])
            contribute(c, minus, near.at[c, 1])

        def part_tile(j, _):
            contract = (((1,), (1,)), ((), ()))
            w_rows = pl.ds(pl.multiple_of(lax.rem(j, 2) * one, one), one)
            value = lax.dot_general(pv[:, :gw], wv[0, j // 2, w_rows, :], contract, preferred_element_type=F32)
            value = value + lax.dot_general(pv[:, gw:], wv[1, j // 2, w_rows, :], contract, preferred_element_type=F32)
            ring[0, :, :, pl.ds(pl.multiple_of(j * one, one), one)] = value.astype(BF).reshape(nz, rows, one)
            return 0

        def part_send(i, _):
            half_i = (i + 1) // 2
            odd = lax.rem(i, 2)
            peer = lax.rem(e + odd * half_i + (1 - odd) * (ne - half_i), ne)
            pltpu.make_async_remote_copy(
                src_ref=ring.at[0, peer // nq, pl.ds(pl.multiple_of(lax.rem(peer, nq) * per, per), per)],
                dst_ref=back.at[e], send_sem=p_send.at[0], recv_sem=p_recv.at[0],
                device_id=(peer, d), device_id_type=MESH).start()
            return 0

        def part_all():
            gate_in.wait()
            lax.fori_loop(0, nd, part_tile, 0)
            lax.fori_loop(1, ne, part_send, 0)
            pltpu.make_async_copy(
                ring.at[0, e // nq, pl.ds(pl.multiple_of(lax.rem(e, nq) * per, per), per)], back.at[e],
                p_local.at[0]).start()

        ring_start(0)
        portion(0)
        hot_wait()
        choose(0, z)
        stage_y(order[0])
        stage_y(order[1])
        ring_step(0, 0)
        ring_start(1)
        stage_x(order[0])
        stage_y(order[2])
        choose(1, z)
        ring_step(0, 1)
        stage_x(order[1])
        stage_r(order[0])
        ring_step(0, 2)
        stage_x(order[2])
        ring_step(0, 3)
        ring_step(1, 0)
        stage_r(order[1])
        down_in()
        rows_in(0)
        experts_back()
        stage_r(order[2])
        ring_step(1, 1)
        start_far(0)
        ring_step(1, 2)
        near_both(0)
        ring_step(1, 3)
        start_near(0)
        for c in order[1:]:
            relayed(c)
        gate_in.start()
        rows_in(1)
        start_far(1)
        start_far(2)
        for c in facts_in:
            c.wait()
        wait_all(ne, [qs], [qv], q_sem.at[pl.ds(0, 1)], q_sem.at[pl.ds(1, 1)], q_local)
        chosen = hev[...] * qv[...].reshape(total, 128)
        grad = jnp.dot(htv[...], chosen, preferred_element_type=F32) + bav[...]
        inner = jnp.sum(pbv[...] * grad, axis=1, keepdims=True)
        grad = pbv[...] * (grad - inner) + exv[...]
        lg[...] = grad
        lg_out = pltpu.make_async_copy(lg, olg, misc.at[3])
        lg_out.start()
        turned = grad.T[:experts]
        high = turned.astype(BF)
        rest = turned - high.astype(F32)
        middle = rest.astype(BF)
        low = (rest - middle.astype(F32)).astype(BF)

        def router_tile(i, _):
            span = pl.ds(pl.multiple_of(i * 512, 512), 512)
            t = tkv[:, span]
            rpart[:, span] = (jnp.dot(low, t, preferred_element_type=F32)
                              + jnp.dot(middle, t, preferred_element_type=F32)
                              + jnp.dot(high, t, preferred_element_type=F32))
            return 0
        lax.fori_loop(0, width // 512, router_tile, 0)

        def rs_dp(i, _):
            q = lax.rem(d + i, nd)
            pltpu.make_async_remote_copy(
                src_ref=rpart.at[pl.ds(pl.multiple_of(q * rp, rp), rp)], dst_ref=rbuf.at[d],
                send_sem=t_send.at[0], recv_sem=t_recv.at[0], device_id=(e, q), device_id_type=MESH).start()
            return 0
        lax.fori_loop(1, nd, rs_dp, 0)
        rbuf[d] = rpart[pl.ds(pl.multiple_of(d * rp, rp), rp), :]

        near_both(1)
        start_near(1)
        pltpu.make_async_remote_copy(
            src_ref=rbuf.at[pl.ds(0, nd - 1)], dst_ref=rbuf.at[pl.ds(0, nd - 1)],
            send_sem=t_send.at[0], recv_sem=t_recv.at[0], device_id=(e, lax.rem(d + 1, nd)),
            device_id_type=MESH).wait()
        racc[...] = jnp.sum(rbuf[...], axis=0)
        mate = e + 1 - 2 * lax.rem(e, 2)
        core = lax.rem(e, 2)
        chip = e // 2
        cc = pltpu.make_async_remote_copy(
            src_ref=racc, dst_ref=rcore, send_sem=t_send.at[1], recv_sem=t_recv.at[1],
            device_id=(mate, d), device_id_type=MESH)
        cc.start()

        cc.wait()
        for n in range(nchip):
            rmine[n] = racc[:, n * rl:(n + 1) * rl] + rcore[:, n * rl:(n + 1) * rl]

        def rs_chip(i, _):
            q = lax.rem(chip + i, nchip)
            pltpu.make_async_remote_copy(
                src_ref=rmine.at[q], dst_ref=rpiece.at[chip], send_sem=t_send.at[2], recv_sem=t_recv.at[2],
                device_id=(q * 2 + core, d), device_id_type=MESH).start()
            return 0
        lax.fori_loop(1, nchip, rs_chip, 0)
        rpiece[chip] = rmine[chip]

        pltpu.make_async_remote_copy(
            src_ref=rpiece.at[pl.ds(0, nchip - 1)], dst_ref=rpiece.at[pl.ds(0, nchip - 1)],
            send_sem=t_send.at[2], recv_sem=t_recv.at[2], device_id=(mate, d), device_id_type=MESH).wait()
        rfull[chip] = jnp.sum(rpiece[...], axis=0)

        def ag_chip(i, _):
            q = lax.rem(chip + i, nchip)
            pltpu.make_async_remote_copy(
                src_ref=rfull.at[chip], dst_ref=rfull.at[chip], send_sem=t_send.at[3], recv_sem=t_recv.at[3],
                device_id=(q * 2 + core, d), device_id_type=MESH).start()
            return 0
        lax.fori_loop(1, nchip, ag_chip, 0)

        part_all()
        near_both(2)
        start_near(2)
        pltpu.make_async_remote_copy(
            src_ref=rfull.at[pl.ds(0, nchip - 1)], dst_ref=rfull.at[pl.ds(0, nchip - 1)],
            send_sem=t_send.at[3], recv_sem=t_recv.at[3], device_id=(mate, d), device_id_type=MESH).wait()

        def ag_dp(i, _):
            q = lax.rem(d + i, nd)
            pltpu.make_async_remote_copy(
                src_ref=rfull, dst_ref=orouter.at[d], send_sem=t_send.at[4], recv_sem=t_recv.at[4],
                device_id=(e, q), device_id_type=MESH).start()
            return 0
        lax.fori_loop(1, nd, ag_dp, 0)
        own_f = pltpu.make_async_copy(rfull, orouter.at[d], misc.at[0])
        own_f.start()

        start_swap(0)
        start_swap(1)
        finish(0)
        start_swap(2)
        finish(1)
        finish(2)

        pltpu.make_async_remote_copy(
            src_ref=orouter.at[pl.ds(0, nd - 1)], dst_ref=orouter.at[pl.ds(0, nd - 1)],
            send_sem=t_send.at[4], recv_sem=t_recv.at[4], device_id=(e, lax.rem(d + 1, nd)),
            device_id_type=MESH).wait()
        own_f.wait()
        lg_out.wait()
        pltpu.make_async_remote_copy(
            src_ref=back.at[pl.ds(0, ne - 1)], dst_ref=back.at[pl.ds(0, ne - 1)],
            send_sem=p_send.at[0], recv_sem=p_recv.at[0], device_id=(mate, d), device_id_type=MESH).wait()
        pltpu.make_async_copy(
            ring.at[0, e // nq, pl.ds(pl.multiple_of(lax.rem(e, nq) * per, per), per)], back.at[e],
            p_local.at[0]).wait()
        for c in range(nc):
            pltpu.make_async_copy(yout.at[c], ow.at[c], fin_sem.at[c]).wait()
        for side, root in ((0, 0), (1, nd - 1)):
            @pl.when(d == root)
            def _():
                pltpu.make_async_remote_copy(
                    src_ref=both.at[side, pl.ds(0, nx - 1)], dst_ref=both.at[side, pl.ds(0, nx - 1)],
                    send_sem=root_send.at[side], recv_sem=piece_sem.at[side, 0],
                    device_id=(e, (root + 2) % nd), device_id_type=MESH).wait_send()

    dma = pltpu.SemaphoreType.DMA
    shape = jax.ShapeDtypeStruct
    vmem = pltpu.VMEM
    return pl.pallas_call(
        kernel,
        out_shape=[shape((2, nx, two, cols), BF), shape((ne, per, width), BF), shape((nc, one, gw), BF),
                   shape((nd, nchip, rp, rl), F32), shape((rows, 128), F32)],
        in_specs=[ANY] * 11, out_specs=[ANY] * 5,
        scratch_shapes=[
            vmem((2, nz, rows, width), BF), vmem((2, slots, rows, width), BF), vmem((nz, nq * per, rows), BF),
            vmem((ne, per, width), BF), vmem((ne, per, width), BF), vmem(saved.shape, BF), vmem(facts.shape, BF),
            vmem((2, nx, two, gw), BF), vmem((total, 2 * gw), BF), vmem((total, gw), BF),
            vmem((ne, per, 128), BF), vmem((ne, per, 128), BF), vmem((total, 128), BF), vmem((rows, total), BF),
            vmem((rows, 128), F32), vmem((1, 128), F32), vmem((rows, 128), F32), vmem((rows, width), BF),
            vmem((rows, 128), F32),
            vmem((nc, two, gw), BF), vmem((nc, 2, two, gw), BF),
            vmem((nc, 2, one, gw), BF), vmem((nc, 2, two, gw), BF), vmem((nc, one, gw), BF), vmem((nc, one, gw), BF),
            vmem((experts, width), F32), vmem((nd, rp, width), F32), vmem((rp, width), F32), vmem((rp, width), F32),
            vmem((nchip, rp, rl), F32), vmem((nchip, rp, rl), F32), vmem((nchip, rp, rl), F32),
            dma((9,)), dma((2,)), dma((2, 2, hops)), dma((2, 2, hops)), dma((2, slots)), dma((2,)), dma((2, slots)),
            dma((2,)), dma((2,)), dma((2,)), dma((2,)), dma((2, nc)), dma((nc,)), dma((nc,)),
            dma((nc, 2)), dma((nc, 2)), dma((nc, 2)), dma((nc, 2)),
            dma((2,)), dma((1,)), dma((1,)), dma((1,)), dma((1,)), dma((nc, 2)), dma((nc, 2)), dma((nc, 2)),
            dma((nc, 2)), dma((nc,)), dma((nc,)),
            dma((5,)), dma((5,)), dma((4,)), dma((nc,))],
        compiler_params=pltpu.CompilerParams(collective_id=1, has_side_effects=True,
                                             vmem_limit_bytes=63 * 1024 * 1024),
    )(tokens, out_grad, saved, facts, pick, weight, hot_expert, hot_token, probs, base, extra)


def local(tokens, out_grad, saved_pre, router_weight, slot_expert, slot_of, slot_weight):
    ne = lax.axis_size("expert")
    nd = lax.axis_size("dp")
    rows, width = tokens.shape
    top = slot_of.shape[1]
    half = saved_pre.shape[2] // 2
    experts = router_weight.shape[1]
    slots = slot_expert.shape[0]
    per = rows * top // ne
    total = rows * top

    group = slot_of // nd
    named = group[:, :, None] == jnp.arange(ne, dtype=jnp.int32)[None, None, :]
    names = jnp.sum(named.astype(F32), axis=1)
    before = (lax.broadcasted_iota(jnp.int32, (rows, rows), 1) < lax.broadcasted_iota(jnp.int32, (rows, rows), 0))
    arrival = jnp.dot(before.astype(BF), names.astype(BF), preferred_element_type=F32)
    rank = jnp.sum(jnp.where(named, arrival[:, None, :], 0.0), axis=2).astype(jnp.int32)
    place = (group * per + rank).reshape(-1)
    perm = place[None, :] == lax.broadcasted_iota(jnp.int32, (total, total), 0)
    perm = perm.astype(BF)
    pick = jnp.sum(perm.reshape(total, rows, top).astype(F32), axis=2).astype(BF)

    slot_hot = slot_of[:, :, None] == jnp.arange(slots, dtype=jnp.int32)[None, None, :]
    expert_ids = jnp.sum(jnp.where(slot_hot, slot_expert[None, None, :], 0), axis=2)
    first_expert = jnp.repeat(slot_expert.reshape(ne, nd)[:, 0], nd)
    is_low = jnp.sum(jnp.where(slot_hot, (slot_expert == first_expert).astype(jnp.int32)[None, None, :], 0), axis=2)

    wide_tokens = tokens.astype(F32)
    logits = jnp.dot(wide_tokens, router_weight, precision=lax.Precision.HIGHEST)
    log_total = jax.nn.logsumexp(logits, axis=1)
    router_probs = jnp.exp(logits - log_total[:, None])
    chosen = expert_ids[:, :, None] == jnp.arange(experts, dtype=jnp.int32)[None, None, :]
    chosen_prob = jnp.sum(jnp.where(chosen, router_probs[:, None, :], 0.0), axis=2).astype(BF)
    counts = jnp.sum(chosen.astype(jnp.int32), axis=(0, 1))

    hot = pick.reshape(2, ne // 4, 2, per, rows).transpose(1, 0, 2, 3, 4).reshape(ne // 4, 4 * per, rows)
    sv_send = jnp.dot(perm, saved_pre.reshape(total, 2 * half), preferred_element_type=F32).astype(BF)
    sv_send = sv_send.reshape(ne, per, 2 * half)
    chosen_row = chosen.reshape(total, experts)
    facts = jnp.concatenate([chosen_prob.reshape(-1, 1), is_low.reshape(-1, 1).astype(BF)], axis=1)
    facts = jnp.pad(facts, ((0, 0), (0, 126)))
    facts = jnp.dot(perm, facts, preferred_element_type=F32).astype(BF).reshape(ne, per, 128)
    wide = ((0, 0), (0, 128 - experts))
    hot_expert = jnp.dot(perm, jnp.pad(chosen_row.astype(BF), wide), preferred_element_type=F32).astype(BF)
    base = (balance_coef * experts * counts.astype(F32) / total)[None, :]
    extra = 2.0 * zloss_coef * log_total[:, None] * router_probs

    _, part_back, sums, router_all, logits_grad = fused(
        tokens, out_grad, sv_send, facts, hot, slot_weight[0], hot_expert, pick.T, jnp.pad(router_probs, wide),
        jnp.pad(base, wide), jnp.pad(extra, wide), ne, nd)
    logits_grad = logits_grad[:, :experts]
    expert_part = lax.dot_general(pick, part_back.reshape(total, width), (((0,), (0,)), ((), ())),
                                  preferred_element_type=F32)
    router_part = jnp.dot(logits_grad, router_weight.T, precision=lax.Precision.HIGHEST)
    token_grad = (expert_part + router_part).astype(BF)
    router_grad = jnp.transpose(router_all, (0, 2, 1, 3)).reshape(experts, width).T

    low_grad = jnp.concatenate([sums[1], sums[0, :, :half]], axis=1)
    high_grad = jnp.concatenate([sums[2], sums[0, :, half:]], axis=1)
    e = lax.axis_index("expert")
    low_first = slot_expert[e * nd] == 2 * e
    expert_grads = jnp.stack([jnp.where(low_first, low_grad, high_grad),
                              jnp.where(low_first, high_grad, low_grad)], axis=1)
    return (token_grad, expert_grads, router_grad)


def solution(mesh):
    placed = (
        P(("expert", "dp"), None),
        P(("expert", "dp"), None),
        P(("expert", "dp"), None, None),
        P(),
        P(),
        P(("expert", "dp"), None),
        P(("expert", "dp"), None, None),
    )
    return jax.shard_map(
        local,
        mesh=mesh,
        in_specs=placed,
        out_specs=(P(("expert", "dp"), None), P("dp", "expert", None), P()),
        check_vma=False,
    )
```

```python
import jax
import jax.numpy as jnp
from jax import lax
from jax.experimental import pallas as pl
from jax.experimental.pallas import tpu as pltpu
from jax.sharding import PartitionSpec as P

zloss_coef = 0.001
balance_coef = 0.01
MESH = pl.DeviceIdType.MESH
ANY = pl.BlockSpec(memory_space=pl.ANY)
BF = jnp.bfloat16
F32 = jnp.float32


def greet(ne, nd, with_expert, with_dp):
    e, d = lax.axis_index("expert"), lax.axis_index("dp")
    barrier = pltpu.get_barrier_semaphore()
    total = 0
    if with_expert:
        def one(i, _):
            pl.semaphore_signal(barrier, inc=1, device_id=(lax.rem(e + i, ne), d), device_id_type=MESH)
            return 0
        lax.fori_loop(1, ne, one, 0)
        total += ne - 1
    if with_dp:
        def two(i, _):
            pl.semaphore_signal(barrier, inc=1, device_id=(e, lax.rem(d + i, nd)), device_id_type=MESH)
            return 0
        lax.fori_loop(1, nd, two, 0)
        total += nd - 1
    pl.semaphore_wait(barrier, total)


def send_all(ne, srcs, dsts, send_sem, recv_sem, local_sem, first=1, last=None):
    e, d = lax.axis_index("expert"), lax.axis_index("dp")
    for n, (src, dst) in enumerate(zip(srcs, dsts)):
        def one(i, _):
            half = (i + 1) // 2
            odd = lax.rem(i, 2)
            off = odd * half + (1 - odd) * (ne - half)
            peer = lax.rem(e + off, ne)
            pltpu.make_async_remote_copy(
                src_ref=src.at[peer], dst_ref=dst.at[e],
                send_sem=send_sem.at[n], recv_sem=recv_sem.at[n],
                device_id=(peer, d), device_id_type=MESH).start()
            return 0
        lax.fori_loop(first, ne if last is None else last, one, 0)
        if first == 1:
            pltpu.make_async_copy(src.at[e], dst.at[e], local_sem.at[n]).start()


def wait_all(ne, srcs, dsts, send_sem, recv_sem, local_sem):
    e, d = lax.axis_index("expert"), lax.axis_index("dp")
    for n, (src, dst) in enumerate(zip(srcs, dsts)):
        pltpu.make_async_remote_copy(
            src_ref=src.at[pl.ds(0, ne - 1)], dst_ref=dst.at[pl.ds(0, ne - 1)],
            send_sem=send_sem.at[n], recv_sem=recv_sem.at[n],
            device_id=(lax.rem(e + 1, ne), d), device_id_type=MESH).wait()
        pltpu.make_async_copy(src.at[e], dst.at[e], local_sem.at[n]).wait()


def fused(tokens, out_grad, saved, facts, pick, weight, hot_expert, hot_token, probs, base, extra, ne, nd):
    rows, width = tokens.shape
    nz = pick.shape[0]
    nq = ne // nz
    per = saved.shape[1]
    half = saved.shape[2] // 2
    total = ne * per
    cols = weight.shape[1]
    wr = width // nd
    nc = 3
    cw = cols // nc
    gw = 2 * cw
    tile = 2048
    hops = nz // 2
    nx = nd // 2
    two = width // nx
    one = width // nd
    experts = 2 * ne
    rp = experts // nd
    nchip = ne // 2
    rl = width // nchip
    st = 32
    slots = 4

    def kernel(tok, og, sv, fa, pk, w, he, ht, pb, ba, ex, both, back, ow, orouter, olg,
               ring, picked, hot, ov, xv, svv, fav, wv, pv, cv, qs, qv, hev, htv, pbv, bav, exv, tkv, lg,
               far, near, got_half, got_full, yout, yin,
               rpart, rbuf, racc, rcore, rmine, rpiece, rfull,
               in_sem, pk_sem, ring_send, ring_recv, sel_send, sel_recv, sel_local,
               send_sem, recv_sem, local_sem, root_send, piece_sem, y_send, y_recv,
               x_send, x_recv, r_send, r_recv,
               q_sem, q_local, p_send, p_recv, p_local, a_send, a_recv, b_send, b_recv, s_send, s_recv,
               t_send, t_recv, misc, fin_sem):
        e, d = lax.axis_index("expert"), lax.axis_index("dp")
        core = lax.rem(e, 2)
        z = lax.rem(e // 2, nz)
        hi = e // (2 * nz)
        quarter = hi * 2 + core

        def at(zz):
            return hi * (2 * nz) + zz * 2 + core

        loads = [pltpu.make_async_copy(og, ring.at[0, z], in_sem.at[0]),
                 pltpu.make_async_copy(tok, ring.at[1, z], in_sem.at[1]),
                 pltpu.make_async_copy(pk.at[z], hot.at[z], in_sem.at[2])]
        facts_in = [pltpu.make_async_copy(s, t, in_sem.at[3 + n]) for n, (s, t) in enumerate(
            ((he, hev), (ht, htv), (pb, pbv), (ba, bav), (ex, exv), (tok, tkv)))]
        for c in loads + facts_in:
            c.start()
        greet(ne, nd, True, True)

        order = (2, 0, 1)
        for side, root in ((0, 0), (1, nd - 1)):
            @pl.when(d == root)
            def _():
                for c in order:
                    span = pl.ds(c * cw, cw)
                    mine = (root // 2) * 2
                    pltpu.make_async_copy(
                        w.at[pl.ds(mine * wr, 2 * wr), span], both.at[side, root // 2, :, span],
                        piece_sem.at[side, c]).start()
                    for j in (1, 3, 2):
                        q = (root // 2 + j) % (nd // 2)
                        pltpu.make_async_remote_copy(
                            src_ref=w.at[pl.ds(q * 2 * wr, 2 * wr), span], dst_ref=both.at[side, q, :, span],
                            send_sem=root_send.at[side], recv_sem=piece_sem.at[side, c],
                            device_id=(e, q * 2 + root % 2), device_id_type=MESH).start()

        def hot_send(i, _):
            q = lax.rem(z + i, nz)
            pltpu.make_async_remote_copy(
                src_ref=pk.at[q], dst_ref=hot.at[z], send_sem=pk_sem.at[0], recv_sem=pk_sem.at[1],
                device_id=(at(q), d), device_id_type=MESH).start()
            return 0
        lax.fori_loop(1, nz, hot_send, 0)

        def ring_copy(n, direction, step):
            sign = 1 - 2 * direction
            block = lax.rem(z - sign * step + nz, nz)
            to = lax.rem(z + sign + nz, nz)
            part = pl.ds(0, rows) if step < hops - 1 else pl.ds(direction * (rows // 2), rows // 2)
            return pltpu.make_async_remote_copy(
                src_ref=ring.at[n, block, part], dst_ref=ring.at[n, block, part],
                send_sem=ring_send.at[n, direction, step], recv_sem=ring_recv.at[n, direction, step],
                device_id=(at(to), d), device_id_type=MESH)

        copies = {(n, g, s): ring_copy(n, g, s) for n in range(2) for g in range(2) for s in range(hops)}

        def rows_out(first, last):
            send_all(ne, [sv, fa], [svv, fav], send_sem, recv_sem, local_sem, first, last)

        def hot_wait():
            loads[2].wait()
            pltpu.make_async_remote_copy(
                src_ref=pk.at[pl.ds(0, nz - 1)], dst_ref=hot.at[pl.ds(0, nz - 1)],
                send_sem=pk_sem.at[0], recv_sem=pk_sem.at[1], device_id=(at(lax.rem(z + 1, nz)), d),
                device_id_type=MESH).wait()

        outs = (ov, xv)
        uses = [0, 0]

        def drain(n, slot):
            some = pl.ds(0, (nq - 1) * per)
            pltpu.make_async_remote_copy(
                src_ref=picked.at[n, slot, some], dst_ref=picked.at[n, slot, some],
                send_sem=sel_send.at[n, slot], recv_sem=sel_recv.at[n], device_id=(at(lax.rem(z + 1, nz)), d),
                device_id_type=MESH).wait_send()
            pltpu.make_async_copy(picked.at[n, slot, pl.ds(0, per)], outs[n].at[0], sel_local.at[n, slot]).wait()

        def choose(n, block):
            slot = uses[n] % slots
            if uses[n] >= slots:
                drain(n, slot)
            uses[n] += 1

            def pick_tile(i, _):
                span = pl.ds(pl.multiple_of(i * tile, tile), tile)
                picked[n, slot, :, span] = jnp.dot(
                    hot[block], ring[n, block, :, span], preferred_element_type=F32).astype(BF)
                return 0
            lax.fori_loop(0, width // tile, pick_tile, 0)
            src_index = at(block)

            def hand(i, _):
                q = lax.rem(quarter + i, nq)
                pltpu.make_async_remote_copy(
                    src_ref=picked.at[n, slot, pl.ds(pl.multiple_of(q * per, per), per)],
                    dst_ref=outs[n].at[src_index], send_sem=sel_send.at[n, slot], recv_sem=sel_recv.at[n],
                    device_id=((q // 2) * (2 * nz) + z * 2 + lax.rem(q, 2), d), device_id_type=MESH).start()
                return 0
            lax.fori_loop(1, nq, hand, 0)
            pltpu.make_async_copy(
                picked.at[n, slot, pl.ds(pl.multiple_of(quarter * per, per), per)],
                outs[n].at[src_index], sel_local.at[n, slot]).start()

        def rows_in(n):
            for slot in range(slots):
                drain(n, slot)
            far_rows = nz * (nq - 1)
            pltpu.make_async_remote_copy(
                src_ref=outs[n].at[pl.ds(0, far_rows)], dst_ref=outs[n].at[pl.ds(0, far_rows)],
                send_sem=sel_send.at[n, 0], recv_sem=sel_recv.at[n], device_id=(at(lax.rem(z + 1, nz)), d),
                device_id_type=MESH).wait_recv()

        pair = d + 1 - 2 * lax.rem(d, 2)
        x, y = d // 2, lax.rem(d, 2)
        nx = nd // 2

        def scattered(c):
            span = pl.ds(c * cw, cw)
            for side in range(2):
                @pl.when(y == side)
                def _():
                    pltpu.make_async_copy(
                        w.at[pl.ds(0, 2 * wr), span], both.at[side, x, :, span], piece_sem.at[side, c]).wait()

        def along_y(c):
            part = both.at[y, x, :, pl.ds(c * cw, cw)]
            return pltpu.make_async_remote_copy(
                src_ref=part, dst_ref=part, send_sem=y_send.at[c], recv_sem=y_recv.at[c],
                device_id=(e, pair), device_id_type=MESH)

        def along_x(c, g):
            part = both.at[pl.ds(0, 2), x, :, pl.ds(c * cw, cw)]
            to = lax.rem(x + 1 + 2 * g, nx)
            return pltpu.make_async_remote_copy(
                src_ref=part, dst_ref=part, send_sem=x_send.at[c, g], recv_sem=x_recv.at[c, g],
                device_id=(e, to * 2 + y), device_id_type=MESH)

        def relay(c, g):
            source = lax.rem(x + 3 - 2 * g, nx)
            part = both.at[g, source, :, pl.ds(c * cw, cw)]
            to = lax.rem(x + 1 + 2 * g, nx)
            return pltpu.make_async_remote_copy(
                src_ref=part, dst_ref=part, send_sem=r_send.at[c, g], recv_sem=r_recv.at[c, g],
                device_id=(e, to * 2 + y), device_id_type=MESH)

        ys = {c: along_y(c) for c in order}
        xs = {(c, g): along_x(c, g) for c in order for g in range(2)}
        rs = {(c, g): relay(c, g) for c in order for g in range(2)}

        def stage_y(c):
            scattered(c)
            ys[c].start()

        def stage_x(c):
            ys[c].wait()
            for g in range(2):
                xs[c, g].start()

        def stage_r(c):
            for g in range(2):
                xs[c, g].wait()
                rs[c, g].start()

        def portion(n):
            rows_out(max(1, n * ne // 4), (n + 1) * ne // 4)

        def ring_start(n):
            loads[n].wait()
            for g in range(2):
                copies[n, g, 0].start()

        def ring_step(n, s):
            for g in range(2):
                copies[n, g, s].wait()
                if s + 1 < hops:
                    copies[n, g, s + 1].start()
            choose(n, lax.rem(z + nz - s - 1, nz))
            if s + 1 < hops:
                choose(n, lax.rem(z + s + 1, nz))

        def relayed(c):
            for g in range(2):
                rs[c, g].wait()

        def down_in():
            relayed(2)
            c = pltpu.make_async_copy(both.at[pl.ds(0, 2), pl.ds(0, nx), :, pl.ds(2 * cw, cw)],
                                      wv.at[pl.ds(0, 2), pl.ds(0, nx), :, pl.ds(0, cw)], misc.at[1])
            c.start()
            c.wait()

        gate_in = pltpu.make_async_copy(both.at[pl.ds(0, 2), pl.ds(0, nx), :, pl.ds(0, gw)], wv, misc.at[2])

        def experts_back():
            wait_all(ne, [sv, fa], [svv, fav], send_sem, recv_sem, local_sem)
            nb = ne // 4

            def block(r, _):
                src = pl.ds(r * nb, nb)
                m = nb * per
                both_back = []
                for side in range(2):
                    value = jnp.zeros((m, half), F32)
                    for j in range(nx):
                        value = value + jnp.dot(ov[src, :, j * two:(j + 1) * two].reshape(m, two),
                                                wv[side, j, :, :half], preferred_element_type=F32)
                    both_back.append(value)
                info = fav[src].reshape(m, 128).astype(F32)
                prob, low = info[:, experts:experts + 1], info[:, experts + 1:experts + 2]
                gradient = jnp.where(low > 0.5, both_back[0], both_back[1])
                saved_rows = svv[src].reshape(m, 2 * half).astype(F32)
                gate, up = saved_rows[:, :half], saved_rows[:, half:]
                sig = 1.0 / (1.0 + jnp.exp(-gate))
                active = gate * sig
                hidden = active * up
                q = jnp.sum(gradient * hidden, axis=1, keepdims=True)
                qs[src] = jnp.broadcast_to(q, (m, 128)).astype(BF).reshape(nb, per, 128)
                scaled = prob * hidden
                grad = prob * gradient
                gate_grad = grad * up * sig * (1.0 + gate * (1.0 - sig))
                up_grad = grad * active
                at_rows = pl.ds(pl.multiple_of(r * m, m), m)
                is_low = low > 0.5
                cv[at_rows, :half] = jnp.where(is_low, scaled, 0.0).astype(BF)
                cv[at_rows, half:] = jnp.where(is_low, 0.0, scaled).astype(BF)
                pv[at_rows, :half] = jnp.where(is_low, gate_grad, 0.0).astype(BF)
                pv[at_rows, half:2 * half] = jnp.where(is_low, up_grad, 0.0).astype(BF)
                pv[at_rows, 2 * half:3 * half] = jnp.where(is_low, 0.0, gate_grad).astype(BF)
                pv[at_rows, 3 * half:] = jnp.where(is_low, 0.0, up_grad).astype(BF)
                return 0
            lax.fori_loop(0, 4, block, 0)
            send_all(ne, [qs], [qv], q_sem.at[pl.ds(0, 1)], q_sem.at[pl.ds(1, 1)], q_local)

        plus, minus, across = lax.rem(x + 1, nx), lax.rem(x + 3, nx), lax.rem(x + 2, nx)

        def product(c, from_row, n):
            left, right, first_col = (ov, cv, 0) if c == 0 else (xv, pv, (c - 1) * gw)
            return lax.dot_general(
                left[:, :, pl.ds(from_row, n)].reshape(total, n), right[:, pl.ds(first_col, gw)],
                (((0,), (0,)), ((), ())), preferred_element_type=F32)

        def contribute(c, target, out):
            def piece(i, _):
                out[pl.ds(pl.multiple_of(i * one, one), one), :] = product(
                    c, pl.multiple_of(target * two + i * one, one), one).astype(BF)
                return 0
            lax.fori_loop(0, 2, piece, 0)

        def first(c, g):
            return pltpu.make_async_remote_copy(
                src_ref=far.at[c, pl.ds(g * one, one)], dst_ref=got_half.at[c, g],
                send_sem=a_send.at[c, g], recv_sem=a_recv.at[c, g],
                device_id=(e, (plus if g == 0 else minus) * 2 + y), device_id_type=MESH)

        def second(c, g):
            return pltpu.make_async_remote_copy(
                src_ref=near.at[c, g], dst_ref=got_full.at[c, g],
                send_sem=b_send.at[c, g], recv_sem=b_recv.at[c, g],
                device_id=(e, (plus if g == 0 else minus) * 2 + y), device_id_type=MESH)

        def swap(c):
            return pltpu.make_async_remote_copy(
                src_ref=yout.at[c], dst_ref=yin.at[c], send_sem=s_send.at[c], recv_sem=s_recv.at[c],
                device_id=(e, d + 1 - 2 * y), device_id_type=MESH)

        firsts = {(c, g): first(c, g) for c in range(nc) for g in range(2)}
        seconds = {(c, g): second(c, g) for c in range(nc) for g in range(2)}
        swaps = [swap(c) for c in range(nc)]

        def start_near(c):
            for g in range(2):
                firsts[c, g].wait()

                def add(i, _):
                    src = pl.ds(pl.multiple_of(i * st, st), st)
                    dst = pl.ds(pl.multiple_of(g * one + i * st, st), st)
                    near[c, g, dst, :] = (near[c, g, dst, :].astype(F32)
                                          + got_half[c, g, src, :].astype(F32)).astype(BF)
                    return 0
                lax.fori_loop(0, one // st, add, 0)
                seconds[c, g].start()

        def summed(c, side, finish):
            def add(i, _):
                src = pl.ds(pl.multiple_of(side * one + i * 128, 128), 128)
                into = pl.ds(pl.multiple_of(i * 128, 128), 128)
                value = product(c, pl.multiple_of(x * two + side * one + i * 128, 128), 128)
                value = value + got_full[c, 0, src, :].astype(F32) + got_full[c, 1, src, :].astype(F32)
                if finish:
                    value = value + yin[c, into, :].astype(F32)
                yout[c, into, :] = value.astype(BF)
                return 0
            lax.fori_loop(0, one // 128, add, 0)

        def start_swap(c):
            for g in range(2):
                seconds[c, g].wait()
            summed(c, 1 - y, False)
            swaps[c].start()

        def finish(c):
            swaps[c].wait()
            summed(c, y, True)
            pltpu.make_async_copy(yout.at[c], ow.at[c], fin_sem.at[c]).start()

        def start_far(c):
            contribute(c, across, far.at[c])
            for g in range(2):
                firsts[c, g].start()

        def near_both(c):
            contribute(c, plus, near.at[c, 0])
            contribute(c, minus, near.at[c, 1])

        def part_tile(j, _):
            contract = (((1,), (1,)), ((), ()))
            w_rows = pl.ds(pl.multiple_of(lax.rem(j, 2) * one, one), one)
            value = lax.dot_general(pv[:, :gw], wv[0, j // 2, w_rows, :], contract, preferred_element_type=F32)
            value = value + lax.dot_general(pv[:, gw:], wv[1, j // 2, w_rows, :], contract, preferred_element_type=F32)
            ring[0, :, :, pl.ds(pl.multiple_of(j * one, one), one)] = value.astype(BF).reshape(nz, rows, one)
            return 0

        def part_send(i, _):
            half_i = (i + 1) // 2
            odd = lax.rem(i, 2)
            peer = lax.rem(e + odd * half_i + (1 - odd) * (ne - half_i), ne)
            pltpu.make_async_remote_copy(
                src_ref=ring.at[0, peer // nq, pl.ds(pl.multiple_of(lax.rem(peer, nq) * per, per), per)],
                dst_ref=back.at[e], send_sem=p_send.at[0], recv_sem=p_recv.at[0],
                device_id=(peer, d), device_id_type=MESH).start()
            return 0

        def part_all():
            gate_in.wait()
            lax.fori_loop(0, nd, part_tile, 0)
            lax.fori_loop(1, ne, part_send, 0)
            pltpu.make_async_copy(
                ring.at[0, e // nq, pl.ds(pl.multiple_of(lax.rem(e, nq) * per, per), per)], back.at[e],
                p_local.at[0]).start()

        ring_start(0)
        portion(0)
        portion(1)
        hot_wait()
        portion(2)
        choose(0, z)
        stage_y(order[0])
        ring_step(0, 0)
        stage_y(order[1])
        stage_x(order[0])
        stage_y(order[2])
        ring_step(0, 1)
        ring_start(1)
        stage_x(order[1])
        ring_step(0, 2)
        stage_r(order[0])
        stage_x(order[2])
        portion(3)
        ring_step(0, 3)
        choose(1, z)
        stage_r(order[1])
        ring_step(1, 0)
        down_in()
        rows_in(0)
        experts_back()
        near_both(0)
        for c in facts_in:
            c.wait()
        wait_all(ne, [qs], [qv], q_sem.at[pl.ds(0, 1)], q_sem.at[pl.ds(1, 1)], q_local)
        chosen = hev[...] * qv[...].reshape(total, 128)
        grad = jnp.dot(htv[...], chosen, preferred_element_type=F32) + bav[...]
        inner = jnp.sum(pbv[...] * grad, axis=1, keepdims=True)
        grad = pbv[...] * (grad - inner) + exv[...]
        lg[...] = grad
        lg_out = pltpu.make_async_copy(lg, olg, misc.at[3])
        lg_out.start()
        turned = grad.T[:experts]
        high = turned.astype(BF)
        rest = turned - high.astype(F32)
        middle = rest.astype(BF)
        low = (rest - middle.astype(F32)).astype(BF)

        def router_tile(i, _):
            span = pl.ds(pl.multiple_of(i * 512, 512), 512)
            t = tkv[:, span]
            rpart[:, span] = (jnp.dot(low, t, preferred_element_type=F32)
                              + jnp.dot(middle, t, preferred_element_type=F32)
                              + jnp.dot(high, t, preferred_element_type=F32))
            return 0
        lax.fori_loop(0, width // 512, router_tile, 0)

        def rs_dp(i, _):
            q = lax.rem(d + i, nd)
            pltpu.make_async_remote_copy(
                src_ref=rpart.at[pl.ds(pl.multiple_of(q * rp, rp), rp)], dst_ref=rbuf.at[d],
                send_sem=t_send.at[0], recv_sem=t_recv.at[0], device_id=(e, q), device_id_type=MESH).start()
            return 0
        lax.fori_loop(1, nd, rs_dp, 0)
        rbuf[d] = rpart[pl.ds(pl.multiple_of(d * rp, rp), rp), :]

        start_far(0)
        ring_step(1, 1)
        pltpu.make_async_remote_copy(
            src_ref=rbuf.at[pl.ds(0, nd - 1)], dst_ref=rbuf.at[pl.ds(0, nd - 1)],
            send_sem=t_send.at[0], recv_sem=t_recv.at[0], device_id=(e, lax.rem(d + 1, nd)),
            device_id_type=MESH).wait()
        racc[...] = jnp.sum(rbuf[...], axis=0)
        mate = e + 1 - 2 * lax.rem(e, 2)
        core = lax.rem(e, 2)
        chip = e // 2
        cc = pltpu.make_async_remote_copy(
            src_ref=racc, dst_ref=rcore, send_sem=t_send.at[1], recv_sem=t_recv.at[1],
            device_id=(mate, d), device_id_type=MESH)
        cc.start()

        stage_r(order[2])
        cc.wait()
        for n in range(nchip):
            rmine[n] = racc[:, n * rl:(n + 1) * rl] + rcore[:, n * rl:(n + 1) * rl]

        def rs_chip(i, _):
            q = lax.rem(chip + i, nchip)
            pltpu.make_async_remote_copy(
                src_ref=rmine.at[q], dst_ref=rpiece.at[chip], send_sem=t_send.at[2], recv_sem=t_recv.at[2],
                device_id=(q * 2 + core, d), device_id_type=MESH).start()
            return 0
        lax.fori_loop(1, nchip, rs_chip, 0)
        rpiece[chip] = rmine[chip]

        ring_step(1, 2)
        start_near(0)
        pltpu.make_async_remote_copy(
            src_ref=rpiece.at[pl.ds(0, nchip - 1)], dst_ref=rpiece.at[pl.ds(0, nchip - 1)],
            send_sem=t_send.at[2], recv_sem=t_recv.at[2], device_id=(mate, d), device_id_type=MESH).wait()
        rfull[chip] = jnp.sum(rpiece[...], axis=0)

        def ag_chip(i, _):
            q = lax.rem(chip + i, nchip)
            pltpu.make_async_remote_copy(
                src_ref=rfull.at[chip], dst_ref=rfull.at[chip], send_sem=t_send.at[3], recv_sem=t_recv.at[3],
                device_id=(q * 2 + core, d), device_id_type=MESH).start()
            return 0
        lax.fori_loop(1, nchip, ag_chip, 0)

        ring_step(1, 3)
        for c in order[1:]:
            relayed(c)
        gate_in.start()
        part_all()
        rows_in(1)
        start_far(1)
        near_both(1)
        start_far(2)
        near_both(2)
        start_near(1)
        start_near(2)
        pltpu.make_async_remote_copy(
            src_ref=rfull.at[pl.ds(0, nchip - 1)], dst_ref=rfull.at[pl.ds(0, nchip - 1)],
            send_sem=t_send.at[3], recv_sem=t_recv.at[3], device_id=(mate, d), device_id_type=MESH).wait()

        def ag_dp(i, _):
            q = lax.rem(d + i, nd)
            pltpu.make_async_remote_copy(
                src_ref=rfull, dst_ref=orouter.at[d], send_sem=t_send.at[4], recv_sem=t_recv.at[4],
                device_id=(e, q), device_id_type=MESH).start()
            return 0
        lax.fori_loop(1, nd, ag_dp, 0)
        own_f = pltpu.make_async_copy(rfull, orouter.at[d], misc.at[0])
        own_f.start()

        start_swap(0)
        start_swap(1)
        finish(0)
        start_swap(2)
        finish(1)
        finish(2)

        pltpu.make_async_remote_copy(
            src_ref=orouter.at[pl.ds(0, nd - 1)], dst_ref=orouter.at[pl.ds(0, nd - 1)],
            send_sem=t_send.at[4], recv_sem=t_recv.at[4], device_id=(e, lax.rem(d + 1, nd)),
            device_id_type=MESH).wait()
        own_f.wait()
        lg_out.wait()
        pltpu.make_async_remote_copy(
            src_ref=back.at[pl.ds(0, ne - 1)], dst_ref=back.at[pl.ds(0, ne - 1)],
            send_sem=p_send.at[0], recv_sem=p_recv.at[0], device_id=(mate, d), device_id_type=MESH).wait()
        pltpu.make_async_copy(
            ring.at[0, e // nq, pl.ds(pl.multiple_of(lax.rem(e, nq) * per, per), per)], back.at[e],
            p_local.at[0]).wait()
        for c in range(nc):
            pltpu.make_async_copy(yout.at[c], ow.at[c], fin_sem.at[c]).wait()
        for side, root in ((0, 0), (1, nd - 1)):
            @pl.when(d == root)
            def _():
                pltpu.make_async_remote_copy(
                    src_ref=both.at[side, pl.ds(0, nx - 1)], dst_ref=both.at[side, pl.ds(0, nx - 1)],
                    send_sem=root_send.at[side], recv_sem=piece_sem.at[side, 0],
                    device_id=(e, (root + 2) % nd), device_id_type=MESH).wait_send()

    dma = pltpu.SemaphoreType.DMA
    shape = jax.ShapeDtypeStruct
    vmem = pltpu.VMEM
    return pl.pallas_call(
        kernel,
        out_shape=[shape((2, nx, two, cols), BF), shape((ne, per, width), BF), shape((nc, one, gw), BF),
                   shape((nd, nchip, rp, rl), F32), shape((rows, 128), F32)],
        in_specs=[ANY] * 11, out_specs=[ANY] * 5,
        scratch_shapes=[
            vmem((2, nz, rows, width), BF), vmem((2, slots, rows, width), BF), vmem((nz, nq * per, rows), BF),
            vmem((ne, per, width), BF), vmem((ne, per, width), BF), vmem(saved.shape, BF), vmem(facts.shape, BF),
            vmem((2, nx, two, gw), BF), vmem((total, 2 * gw), BF), vmem((total, gw), BF),
            vmem((ne, per, 128), BF), vmem((ne, per, 128), BF), vmem((total, 128), BF), vmem((rows, total), BF),
            vmem((rows, 128), F32), vmem((1, 128), F32), vmem((rows, 128), F32), vmem((rows, width), BF),
            vmem((rows, 128), F32),
            vmem((nc, two, gw), BF), vmem((nc, 2, two, gw), BF),
            vmem((nc, 2, one, gw), BF), vmem((nc, 2, two, gw), BF), vmem((nc, one, gw), BF), vmem((nc, one, gw), BF),
            vmem((experts, width), F32), vmem((nd, rp, width), F32), vmem((rp, width), F32), vmem((rp, width), F32),
            vmem((nchip, rp, rl), F32), vmem((nchip, rp, rl), F32), vmem((nchip, rp, rl), F32),
            dma((9,)), dma((2,)), dma((2, 2, hops)), dma((2, 2, hops)), dma((2, slots)), dma((2,)), dma((2, slots)),
            dma((2,)), dma((2,)), dma((2,)), dma((2,)), dma((2, nc)), dma((nc,)), dma((nc,)),
            dma((nc, 2)), dma((nc, 2)), dma((nc, 2)), dma((nc, 2)),
            dma((2,)), dma((1,)), dma((1,)), dma((1,)), dma((1,)), dma((nc, 2)), dma((nc, 2)), dma((nc, 2)),
            dma((nc, 2)), dma((nc,)), dma((nc,)),
            dma((5,)), dma((5,)), dma((4,)), dma((nc,))],
        compiler_params=pltpu.CompilerParams(collective_id=1, has_side_effects=True,
                                             vmem_limit_bytes=63 * 1024 * 1024),
    )(tokens, out_grad, saved, facts, pick, weight, hot_expert, hot_token, probs, base, extra)


def local(tokens, out_grad, saved_pre, router_weight, slot_expert, slot_of, slot_weight):
    ne = lax.axis_size("expert")
    nd = lax.axis_size("dp")
    rows, width = tokens.shape
    top = slot_of.shape[1]
    half = saved_pre.shape[2] // 2
    experts = router_weight.shape[1]
    slots = slot_expert.shape[0]
    per = rows * top // ne
    total = rows * top

    group = slot_of // nd
    named = group[:, :, None] == jnp.arange(ne, dtype=jnp.int32)[None, None, :]
    names = jnp.sum(named.astype(F32), axis=1)
    before = (lax.broadcasted_iota(jnp.int32, (rows, rows), 1) < lax.broadcasted_iota(jnp.int32, (rows, rows), 0))
    arrival = jnp.dot(before.astype(BF), names.astype(BF), preferred_element_type=F32)
    rank = jnp.sum(jnp.where(named, arrival[:, None, :], 0.0), axis=2).astype(jnp.int32)
    place = (group * per + rank).reshape(-1)
    perm = place[None, :] == lax.broadcasted_iota(jnp.int32, (total, total), 0)
    perm = perm.astype(BF)
    pick = jnp.sum(perm.reshape(total, rows, top).astype(F32), axis=2).astype(BF)

    first_expert = jnp.repeat(slot_expert.reshape(ne, nd)[:, 0], nd)
    lane = jnp.arange(128, dtype=jnp.int32)[None, :]
    table = (lane == slot_expert[:, None]) | ((lane == experts + 1) & (slot_expert == first_expert)[:, None])
    slot_hot = slot_of.reshape(-1, 1) == jnp.arange(slots, dtype=jnp.int32)[None, :]
    info = jnp.dot(slot_hot.astype(BF), table.astype(BF), preferred_element_type=F32)

    wide_tokens = tokens.astype(F32)
    logits = jnp.dot(wide_tokens, router_weight, precision=lax.Precision.HIGHEST)
    log_total = jax.nn.logsumexp(logits, axis=1)
    router_probs = jnp.exp(logits - log_total[:, None])
    wide = ((0, 0), (0, 128 - experts))
    wide_probs = jnp.pad(router_probs, wide)
    chosen_prob = jnp.sum(info.reshape(rows, top, 128) * wide_probs[:, None, :], axis=2)
    counts = jnp.sum(info, axis=0)[:experts]

    hot = pick.reshape(2, ne // 4, 2, per, rows).transpose(1, 0, 2, 3, 4).reshape(ne // 4, 4 * per, rows)
    sv_send = jnp.dot(perm, saved_pre.reshape(total, 2 * half), preferred_element_type=F32).astype(BF)
    sv_send = sv_send.reshape(ne, per, 2 * half)
    facts = jnp.where(lane == experts, chosen_prob.reshape(-1, 1), info).astype(BF)
    facts = jnp.dot(perm, facts, preferred_element_type=F32).astype(BF)
    base = (balance_coef * experts * counts / total)[None, :]
    extra = 2.0 * zloss_coef * log_total[:, None] * router_probs

    _, part_back, sums, router_all, logits_grad = fused(
        tokens, out_grad, sv_send, facts.reshape(ne, per, 128), hot, slot_weight[0], facts, pick.T, wide_probs,
        jnp.pad(base, wide), jnp.pad(extra, wide), ne, nd)
    logits_grad = logits_grad[:, :experts]
    expert_part = lax.dot_general(pick, part_back.reshape(total, width), (((0,), (0,)), ((), ())),
                                  preferred_element_type=F32)
    router_part = jnp.dot(logits_grad, router_weight.T, precision=lax.Precision.HIGHEST)
    token_grad = (expert_part + router_part).astype(BF)
    router_grad = jnp.transpose(router_all, (0, 2, 1, 3)).reshape(experts, width).T

    low_grad = jnp.concatenate([sums[1], sums[0, :, :half]], axis=1)
    high_grad = jnp.concatenate([sums[2], sums[0, :, half:]], axis=1)
    e = lax.axis_index("expert")
    low_first = slot_expert[e * nd] == 2 * e
    expert_grads = jnp.stack([jnp.where(low_first, low_grad, high_grad),
                              jnp.where(low_first, high_grad, low_grad)], axis=1)
    return (token_grad, expert_grads, router_grad)


def solution(mesh):
    placed = (
        P(("expert", "dp"), None),
        P(("expert", "dp"), None),
        P(("expert", "dp"), None, None),
        P(),
        P(),
        P(("expert", "dp"), None),
        P(("expert", "dp"), None, None),
    )
    return jax.shard_map(
        local,
        mesh=mesh,
        in_specs=placed,
        out_specs=(P(("expert", "dp"), None), P("dp", "expert", None), P()),
        check_vma=False,
    )
```
